512 devices in a mesh: row: 16 (over x_lo, y, core), col: 32 (over x_hi, z).
Axes of the slice: x: 4 (x_hi: 2, x_lo: 2; x = x_hi * 2 + x_lo), y: 4, z: 16, core: 2. Of those that a mesh axis runs over, the one named last changes fastest.
Arguments:
- matrix: float32 [8, 16, 128, 4, 32, 128], P(None, 'row', None, None, 'col'), may hold values from -8.5 to 8.5
- vectors: float32 [2, 8, 16, 128, 96], P(None, None, 'row', 'col'), may hold values from -0.046875 to 0.046875
- factors: float32 [2, 96, 96], replicated, may hold values from -0.30618622 to 1.6, as said below
Outputs:
- updated: float32 [8, 16, 128, 4, 32, 128], P(None, 'row', None, None, 'col')
The draws below stay inside these ranges and needn't reach their ends.
Inputs may be any that keep to these rules, and one draw needn't show every extreme that they name: Each factors[k] is upper triangular with a positive diagonal.
All inputs are finite; a program needn't handle non-finite values.
Results may differ from the reference program's by a relative error of at most 0.0001.
Values sent between devices are 32-bit elements; how exact they have to be, the bound alone decides.
No kernel may reach another device: no remote copies, remote signals or barrier semaphores. Data moves between devices by JAX's collectives and lax.ppermute only.
A program may use at most 64 MiB of HBM per device.

```python
import math
import jax
import jax.numpy as jnp
from jax import lax

N = 16384
TB = 128
PW = 96
PANELS = 2
LT = 8
LC = 4
N_ROW = 16
N_COL = 32


def draw_matrix(key, part):
    random_part = jnp.clip(jax.random.normal(key, (N, N), jnp.float32), -6.0, 6.0)
    symmetric = (random_part + random_part.T) * 0.7071
    return symmetric.reshape(LT, N_ROW, TB, LC, N_COL, TB)


def draw_factors(key, part):
    first_key = jax.random.fold_in(key, 11)
    second_key = jax.random.fold_in(key, 12)
    upper = jnp.clip(jax.random.normal(first_key, (PANELS, PW, PW), jnp.float32), -6.0, 6.0) * (0.5 / math.sqrt(PW))
    diagonal = jax.random.uniform(second_key, (PANELS, PW), jnp.float32, 0.8, 1.6)
    strict = jnp.triu(jnp.ones((PW, PW), jnp.float32), 1)
    return upper * strict + diagonal[:, :, None] * jnp.eye(PW, dtype=jnp.float32)


def block_levels(own_key, dims, cuts, least, top_value):
    def one(axis_at, blocks):
        draws = jax.random.uniform(jax.random.fold_in(jax.random.fold_in(own_key, 6), axis_at), (blocks,), jnp.float32, least / len(cuts), top_value / len(cuts))
        return jnp.repeat(jnp.exp(draws), dims[axis_at] // blocks).reshape((-1,) + (1,) * (len(dims) - axis_at - 1))

    factor_of = one(*cuts[0])
    for cut in cuts[1:]:
        factor_of = factor_of * one(*cut)
    return factor_of


def gaussian(stream_key, dims, width, most, pieces=(), kind=jnp.bfloat16):
    values = jax.random.normal(stream_key, dims, jnp.float32) * width
    if len(pieces) > 0:
        values = block_levels(stream_key, dims, pieces, -0.22, 0.18) * values
    return jnp.clip(values, min=-most, max=most).astype(kind)


def setup_inputs(seed: int = 0) -> dict:
    key_of = jax.random.split(jax.random.key(seed), 4)
    return {
        "matrix": draw_matrix(jax.random.fold_in(key_of[3], 71), 0),
        "vectors": gaussian(key_of[1], (PANELS, LT, N_ROW, TB, PW), N ** -0.5, 0.046875, ((2, 16), (3, 32)), jnp.float32),
        "factors": draw_factors(jax.random.fold_in(key_of[3], 71), 0),
    }


def product(matrix_a, matrix_b):
    return jnp.dot(matrix_a, matrix_b, precision=lax.Precision.HIGHEST, preferred_element_type=jnp.float32)


def reference(matrix, vectors, factors):
    current = matrix.reshape(N, N)
    for number in range(PANELS):
        basis = vectors[number].reshape(N, PW)
        factor = factors[number]
        update = product(product(current, basis), factor)
        correlation = product(basis.T, update)
        update = update - 0.5 * product(basis, product(factor.T, correlation))
        current = current - product(basis, update.T) - product(update, basis.T)
    return current.reshape(matrix.shape)
```

```python
import jax
import jax.numpy as jnp
from jax import lax
from jax.experimental import pallas as pl
from jax.experimental.pallas import tpu as pltpu
from jax.sharding import Mesh
from jax.sharding import PartitionSpec as P

ROWS = 16
ZS = 16
XS = 2
W = 96
LANES = 128
SLICE = 48
PART = 24
BLOCK = 72


def dot(a, b, ca=1, cb=0):
    return lax.dot_general(
        a,
        b,
        (((ca,), (cb,)), ((), ())),
        precision=lax.Precision.HIGHEST,
        preferred_element_type=jnp.float32,
    )


def call(kernel, outs, scratch, flops, *args):
    shapes = [jax.ShapeDtypeStruct(s, jnp.float32) for s in outs]
    moved = sum(x.size for x in list(args) + shapes) * 4
    return pl.pallas_call(
        kernel,
        out_shape=shapes,
        in_specs=[pl.BlockSpec(memory_space=pltpu.VMEM)] * len(args),
        out_specs=[pl.BlockSpec(memory_space=pltpu.VMEM)] * len(outs),
        scratch_shapes=[pltpu.VMEM(s, jnp.float32) for s in scratch],
        compiler_params=pltpu.CompilerParams(vmem_limit_bytes=40 * 1024 * 1024),
        cost_estimate=pl.CostEstimate(flops=flops, bytes_accessed=moved, transcendentals=0),
    )(*args)


def pack_kernel(v_ref, all_ref, own_ref, other_ref):
    xh = lax.axis_index("xh")
    first = [jnp.concatenate([v_ref[0, i], v_ref[1, i][:, :32]], axis=1) for i in range(8)]
    rest = [v_ref[1, i][:, 32:] for i in range(8)]
    pairs = [jnp.concatenate([rest[i], rest[i + 4]], axis=1) for i in range(4)]
    block = jnp.concatenate(first + pairs, axis=0)
    for k in range(ZS):
        all_ref[k] = block
    halves = []
    for h in range(2):
        low = [jnp.concatenate([rest[2 * j + h], rest[2 * j + 4 + h]], axis=1) for j in range(2)]
        halves.append(jnp.concatenate([first[2 * j + h] for j in range(4)] + low, axis=0))
    is_low = xh == 0
    own_ref[...] = jnp.where(is_low, halves[0], halves[1])
    other_ref[...] = jnp.where(is_low, halves[1], halves[0])


def image_kernel(a_ref, g_ref, own_ref, other_ref, send_ref, va_ref, vb_ref):
    xh = lax.axis_index("xh")
    for i in range(8):
        for r in range(4):
            va_ref[pl.ds(i * 128 + r, 32, stride=4), :] = g_ref[
                pl.ds(i * 4 + r, 32, stride=SLICE), :
            ]
    for i in range(4):
        for r in range(4):
            both = g_ref[pl.ds(32 + i * 4 + r, 32, stride=SLICE), :]
            vb_ref[pl.ds(i * 128 + r, 32, stride=4), :] = both
            vb_ref[pl.ds((i + 4) * 128 + r, 32, stride=4), :] = pltpu.roll(both, 64, 1)
    v = jnp.concatenate([va_ref[...], vb_ref[:, :64]], axis=1)
    for half in range(2):
        tiles = [a_ref[pl.ds(2 * half + t, 1024, stride=4), :] for t in range(2)]
        q = dot(v, jnp.concatenate(tiles, axis=1), 0, 0)
        for t in range(2):
            j = 2 * half + t
            for kk in range(12):
                send_ref[pl.ds(kk * 4 + j, 16, stride=2 * SLICE), :] = q[
                    kk * 16 : kk * 16 + 16, t * 128 : t * 128 + 128
                ]
    is_low = xh == 0
    zero = jnp.where(is_low, own_ref[...], other_ref[...])
    one = jnp.where(is_low, other_ref[...], own_ref[...])
    for k in range(ROWS):
        send_ref[k * 96 + 48 : k * 96 + 72, :] = zero
        send_ref[k * 96 + 72 : k * 96 + 96, :] = one


def slice_kernel(r_ref, block_ref, y_ref, va_ref, vb_ref, sum_ref):
    me = lax.axis_index("row")
    total = r_ref[0:48, :]
    for k in range(1, ROWS):
        total = total + r_ref[k * 96 : k * 96 + 48, :]
    sum_ref[...] = total
    for x in range(XS):
        for j in range(4):
            for r in range(4):
                va_ref[pl.ds(j * 128 + x * 64 + r, 16, stride=4), :] = r_ref[
                    pl.ds(48 + x * 24 + j * 4 + r, 16, stride=96), :
                ]
        for j in range(2):
            for r in range(4):
                both = r_ref[pl.ds(64 + x * 24 + j * 4 + r, 16, stride=96), :]
                vb_ref[pl.ds(j * 128 + x * 64 + r, 16, stride=4), :] = both
                vb_ref[pl.ds((j + 2) * 128 + x * 64 + r, 16, stride=4), :] = pltpu.roll(both, 64, 1)
    v = jnp.concatenate([va_ref[...], vb_ref[:, :64]], axis=1)
    y = jnp.concatenate([sum_ref[pl.ds(j, 12, stride=4), :] for j in range(4)], axis=1)
    ht = dot(y, v)
    gram = dot(v[:, :W], v[:, W:], 0, 0)
    at = lax.broadcasted_iota(jnp.int32, (8, W), 0) * 16 + me
    pick = jnp.where(at == lax.broadcasted_iota(jnp.int32, (8, W), 1), 1.0, 0.0)
    mine = dot(pick, gram)
    low = jnp.concatenate([ht[0:6, 128:], ht[6:12, 128:]], axis=1)
    mine = jnp.concatenate([mine[0:6], jnp.zeros((6, 32), jnp.float32)], axis=1)
    tail = jnp.concatenate([ht[:, :128], low, mine], axis=0)
    for k in range(ZS):
        block_ref[k, 0:48, :] = total
        block_ref[k, 48:72, :] = tail
        y_ref[k] = total


def turn_kernel(r_ref, out_ref):
    tail = r_ref[0, 48:72, :]
    for k in range(1, ZS):
        tail = tail + r_ref[k, 48:72, :]
    for k in range(ROWS):
        for x in range(XS):
            out_ref[2 * k + x, 0:48, :] = r_ref[k, 0:48, :]
            out_ref[2 * k + x, 48:72, :] = tail


def update_kernel(
    a_ref, vra_ref, vrb_ref, vca_ref, vcb_ref, y_ref, r_ref, t_ref, out_ref, yr_ref, yc_ref
):
    def both(start):
        here = r_ref[pl.ds(start, 16, stride=2 * BLOCK), :]
        return here + r_ref[pl.ds(start + BLOCK, 16, stride=2 * BLOCK), :]

    wide = [both(48 + k) for k in range(12)]
    low = [both(60 + k) for k in range(6)]
    h_a = jnp.concatenate(wide, axis=0)
    h_b = jnp.concatenate([x[:, :64] for x in low] + [x[:, 64:] for x in low], axis=0)
    ht = jnp.concatenate([h_a, h_b], axis=1)
    g = jnp.concatenate([both(66 + k) for k in range(6)], axis=0)[:, :W]
    for k in range(12):
        for j in range(4):
            for x in range(XS):
                i = 2 * j + x
                yr_ref[k * 16 : k * 16 + 16, i * 128 : i * 128 + 128] = r_ref[
                    pl.ds(x * BLOCK + k * 4 + j, 16, stride=2 * BLOCK), :
                ]
            yc_ref[k * 16 : k * 16 + 16, j * 128 : j * 128 + 128] = y_ref[
                pl.ds(k * 4 + j, 16, stride=SLICE), :
            ]
    t1 = t_ref[0]
    t2 = t_ref[1]
    shift1 = 0.5 * dot(t1, dot(ht[:W, :W], t1), 0, 0)
    crossed = dot(t1, ht[:W, W:], 0, 0) - dot(shift1, g, 0, 0)
    fold = dot(g, crossed, 0, 0)
    second = ht[W:, W:] - fold - fold.T
    shift2 = 0.5 * dot(t2, dot(second, t2), 0, 0)
    gt = dot(g, t2)
    corner = dot(crossed, t2) - dot(shift1, gt)
    none = jnp.zeros((W, W), jnp.float32)
    left = jnp.concatenate(
        [
            jnp.concatenate([t1, -dot(t1, gt)], axis=1),
            jnp.concatenate([none, t2], axis=1),
        ],
        axis=0,
    )
    sym = jnp.concatenate(
        [
            jnp.concatenate([shift1 + shift1.T, corner], axis=1),
            jnp.concatenate([corner.T, shift2 + shift2.T], axis=1),
        ],
        axis=0,
    )
    vc = jnp.concatenate([vca_ref[...], vcb_ref[:, :64]], axis=1)
    m1 = dot(left, yc_ref[...], 0, 0) - dot(sym, vc, 1, 1)
    m2 = dot(left, vc, 1, 1)
    for i in range(8):
        at = i * 128
        vr = jnp.concatenate([vra_ref[at : at + 128, :], vrb_ref[at : at + 128, :64]], axis=1)
        change = dot(vr, m1) + dot(yr_ref[:, at : at + 128], m2, 0, 0)
        for j in range(4):
            where = pl.ds(at * 4 + j, 128, stride=4)
            out_ref[where, :] = a_ref[where, :] - change[:, j * 128 : j * 128 + 128]


def spread(array, axes):
    return lax.all_to_all(array, axes, split_axis=0, concat_axis=0, tiled=True)


def shards(matrix, vectors, factors):
    blocks = matrix.reshape(-1, LANES)
    every = [(p, x, z) for p in range(ROWS) for x in range(XS) for z in range(ZS)]
    number = {at: k for k, at in enumerate(every)}
    same = [(number[p, x, z], number[z, x, p]) for p, x, z in every]
    cross = [(number[p, x, z], number[z, 1 - x, p]) for p, x, z in every]
    whole = ("row", "xh", "z")

    sent, own, other = call(
        pack_kernel,
        [(ZS, SLICE, LANES), (PART, LANES), (PART, LANES)],
        [],
        0,
        vectors.reshape(2, 8, 4, W),
    )
    own = lax.ppermute(own, whole, same)
    other = lax.ppermute(other, whole, cross)
    column = spread(sent, "z").reshape(ZS * SLICE, LANES)
    gathered = lax.all_gather(column, "xh", axis=0, tiled=True)
    image, vra, vrb = call(
        image_kernel,
        [(ROWS * 96, LANES), (1024, LANES), (1024, LANES)],
        [],
        2 * 1024 * 512 * 192,
        blocks,
        gathered,
        own,
        other,
    )
    image = spread(image.reshape(ROWS, 96, LANES), "row").reshape(-1, LANES)
    block, mine, vca, vcb = call(
        slice_kernel,
        [(ZS, BLOCK, LANES), (ROWS, SLICE, LANES), (512, LANES), (512, LANES)],
        [(SLICE, LANES)],
        2 * 512 * 192 * 96,
        image,
    )
    y_cols = spread(mine, "row").reshape(-1, LANES)
    block = spread(block, "z")
    (block,) = call(turn_kernel, [(2 * ROWS, BLOCK, LANES)], [], 0, block)
    y_rows = spread(block, ("row", "xh")).reshape(-1, LANES)
    (out,) = call(
        update_kernel,
        [(4096, LANES)],
        [(192, 1024), (192, 512)],
        2 * 1024 * 512 * 384,
        blocks,
        vra,
        vrb,
        vca,
        vcb,
        y_cols,
        y_rows,
        factors,
    )
    return out.reshape(matrix.shape)


def solution(mesh):
    finer = Mesh(mesh.devices.reshape(ROWS, XS, ZS), ("row", "xh", "z"))
    cols = ("xh", "z")
    placed = (P(None, "row", None, None, cols, None), P(None, None, "row", cols, None), P())
    return jax.shard_map(
        shards,
        mesh=finer,
        in_specs=placed,
        out_specs=placed[0],
        check_vma=False,
    )
```

```python
import jax
import jax.numpy as jnp
from jax import lax
from jax.experimental import pallas as pl
from jax.experimental.pallas import tpu as pltpu
from jax.sharding import Mesh
from jax.sharding import PartitionSpec as P

ROWS = 16
ZS = 16
XS = 2
W = 96
LANES = 128
SLICE = 48
PART = 24
BLOCK = 72


def dot(a, b, ca=1, cb=0):
    return lax.dot_general(
        a,
        b,
        (((ca,), (cb,)), ((), ())),
        precision=lax.Precision.HIGHEST,
        preferred_element_type=jnp.float32,
    )


def call(kernel, outs, scratch, flops, *args):
    shapes = [jax.ShapeDtypeStruct(s, jnp.float32) for s in outs]
    moved = sum(x.size for x in list(args) + shapes) * 4
    return pl.pallas_call(
        kernel,
        out_shape=shapes,
        in_specs=[pl.BlockSpec(memory_space=pltpu.VMEM)] * len(args),
        out_specs=[pl.BlockSpec(memory_space=pltpu.VMEM)] * len(outs),
        scratch_shapes=[pltpu.VMEM(s, jnp.float32) for s in scratch],
        compiler_params=pltpu.CompilerParams(vmem_limit_bytes=40 * 1024 * 1024),
        cost_estimate=pl.CostEstimate(flops=flops, bytes_accessed=moved, transcendentals=0),
    )(*args)


def pack_kernel(v_ref, out_ref):
    first = [jnp.concatenate([v_ref[0, i], v_ref[1, i][:, :32]], axis=1) for i in range(8)]
    rest = [v_ref[1, i][:, 32:] for i in range(8)]
    parts = []
    for h in range(2):
        parts += [first[2 * j + h] for j in range(4)]
        parts += [
            jnp.concatenate([rest[2 * j + h], rest[2 * j + 4 + h]], axis=1) for j in range(2)
        ]
    out_ref[...] = jnp.concatenate(parts, axis=0)


def image_kernel(a_ref, g_ref, own_ref, send_ref, va_ref, vb_ref):
    for x in range(XS):
        for j in range(4):
            for h in range(2):
                for r in range(4):
                    to = pl.ds((2 * j + h) * 128 + x * 64 + r, 16, stride=4)
                    va_ref[to, :] = g_ref[
                        pl.ds(x * SLICE + h * PART + j * 4 + r, 16, stride=2 * SLICE), :
                    ]
        for j in range(2):
            for h in range(2):
                for r in range(4):
                    both = g_ref[
                        pl.ds(x * SLICE + h * PART + 16 + j * 4 + r, 16, stride=2 * SLICE), :
                    ]
                    at = (2 * j + h) * 128 + x * 64 + r
                    vb_ref[pl.ds(at, 16, stride=4), :] = both
                    vb_ref[pl.ds(at + 512, 16, stride=4), :] = pltpu.roll(both, 64, 1)
    v = jnp.concatenate([va_ref[...], vb_ref[:, :64]], axis=1)
    for half in range(2):
        tiles = [a_ref[pl.ds(2 * half + t, 1024, stride=4), :] for t in range(2)]
        q = dot(v, jnp.concatenate(tiles, axis=1), 0, 0)
        for t in range(2):
            j = 2 * half + t
            for kk in range(12):
                send_ref[pl.ds(kk * 4 + j, 16, stride=2 * SLICE), :] = q[
                    kk * 16 : kk * 16 + 16, t * 128 : t * 128 + 128
                ]
    own = own_ref[...]
    for k in range(ROWS):
        send_ref[k * 96 + 48 : k * 96 + 96, :] = own


def slice_kernel(r_ref, block_ref, y_ref, va_ref, vb_ref, sum_ref):
    me = lax.axis_index("row")
    total = r_ref[0:48, :]
    for k in range(1, ROWS):
        total = total + r_ref[k * 96 : k * 96 + 48, :]
    sum_ref[...] = total
    for x in range(XS):
        for j in range(4):
            for r in range(4):
                va_ref[pl.ds(j * 128 + x * 64 + r, 16, stride=4), :] = r_ref[
                    pl.ds(48 + x * 24 + j * 4 + r, 16, stride=96), :
                ]
        for j in range(2):
            for r in range(4):
                both = r_ref[pl.ds(64 + x * 24 + j * 4 + r, 16, stride=96), :]
                vb_ref[pl.ds(j * 128 + x * 64 + r, 16, stride=4), :] = both
                vb_ref[pl.ds((j + 2) * 128 + x * 64 + r, 16, stride=4), :] = pltpu.roll(both, 64, 1)
    v = jnp.concatenate([va_ref[...], vb_ref[:, :64]], axis=1)
    y = jnp.concatenate([sum_ref[pl.ds(j, 12, stride=4), :] for j in range(4)], axis=1)
    ht = dot(y, v)
    gram = dot(v[:, :W], v[:, W:], 0, 0)
    at = lax.broadcasted_iota(jnp.int32, (8, W), 0) * 16 + me
    pick = jnp.where(at == lax.broadcasted_iota(jnp.int32, (8, W), 1), 1.0, 0.0)
    mine = dot(pick, gram)
    low = jnp.concatenate([ht[0:6, 128:], ht[6:12, 128:]], axis=1)
    mine = jnp.concatenate([mine[0:6], jnp.zeros((6, 32), jnp.float32)], axis=1)
    tail = jnp.concatenate([ht[:, :128], low, mine], axis=0)
    block_ref[0:48, :] = total
    block_ref[48:72, :] = tail
    for k in range(ROWS):
        y_ref[k] = total


def turn_kernel(r_ref, out_ref):
    tail = r_ref[0, 48:72, :]
    for k in range(1, ZS):
        tail = tail + r_ref[k, 48:72, :]
    for k in range(ROWS):
        for x in range(XS):
            out_ref[2 * k + x, 0:48, :] = r_ref[k, 0:48, :]
            out_ref[2 * k + x, 48:72, :] = tail


def update_kernel(
    a_ref, vra_ref, vrb_ref, vca_ref, vcb_ref, y_ref, r_ref, t_ref, out_ref, yr_ref, yc_ref
):
    def both(start):
        here = r_ref[pl.ds(start, 16, stride=2 * BLOCK), :]
        return here + r_ref[pl.ds(start + BLOCK, 16, stride=2 * BLOCK), :]

    wide = [both(48 + k) for k in range(12)]
    low = [both(60 + k) for k in range(6)]
    h_a = jnp.concatenate(wide, axis=0)
    h_b = jnp.concatenate([x[:, :64] for x in low] + [x[:, 64:] for x in low], axis=0)
    ht = jnp.concatenate([h_a, h_b], axis=1)
    g = jnp.concatenate([both(66 + k) for k in range(6)], axis=0)[:, :W]
    for k in range(12):
        for j in range(4):
            for x in range(XS):
                i = 2 * j + x
                yr_ref[k * 16 : k * 16 + 16, i * 128 : i * 128 + 128] = r_ref[
                    pl.ds(x * BLOCK + k * 4 + j, 16, stride=2 * BLOCK), :
                ]
            yc_ref[k * 16 : k * 16 + 16, j * 128 : j * 128 + 128] = y_ref[
                pl.ds(k * 4 + j, 16, stride=SLICE), :
            ]
    t1 = t_ref[0]
    t2 = t_ref[1]
    shift1 = 0.5 * dot(t1, dot(ht[:W, :W], t1), 0, 0)
    crossed = dot(t1, ht[:W, W:], 0, 0) - dot(shift1, g, 0, 0)
    fold = dot(g, crossed, 0, 0)
    second = ht[W:, W:] - fold - fold.T
    shift2 = 0.5 * dot(t2, dot(second, t2), 0, 0)
    gt = dot(g, t2)
    corner = dot(crossed, t2) - dot(shift1, gt)
    none = jnp.zeros((W, W), jnp.float32)
    left = jnp.concatenate(
        [
            jnp.concatenate([t1, -dot(t1, gt)], axis=1),
            jnp.concatenate([none, t2], axis=1),
        ],
        axis=0,
    )
    sym = jnp.concatenate(
        [
            jnp.concatenate([shift1 + shift1.T, corner], axis=1),
            jnp.concatenate([corner.T, shift2 + shift2.T], axis=1),
        ],
        axis=0,
    )
    vc = jnp.concatenate([vca_ref[...], vcb_ref[:, :64]], axis=1)
    m1 = dot(left, yc_ref[...], 0, 0) - dot(sym, vc, 1, 1)
    m2 = dot(left, vc, 1, 1)
    for i in range(8):
        at = i * 128
        vr = jnp.concatenate([vra_ref[at : at + 128, :], vrb_ref[at : at + 128, :64]], axis=1)
        change = dot(vr, m1) + dot(yr_ref[:, at : at + 128], m2, 0, 0)
        for j in range(4):
            where = pl.ds(at * 4 + j, 128, stride=4)
            out_ref[where, :] = a_ref[where, :] - change[:, j * 128 : j * 128 + 128]


def spread(array, axes):
    return lax.all_to_all(array, axes, split_axis=0, concat_axis=0, tiled=True)


def shards(matrix, vectors, factors):
    blocks = matrix.reshape(-1, LANES)
    every = [(p, x, z) for p in range(ROWS) for x in range(XS) for z in range(ZS)]
    number = {at: k for k, at in enumerate(every)}
    same = [(number[p, x, z], number[z, x, p]) for p, x, z in every]
    whole = ("row", "xh", "z")

    (packed,) = call(pack_kernel, [(SLICE, LANES)], [], 0, vectors.reshape(2, 8, 4, W))
    pair = lax.all_gather(packed, "xh")
    own = lax.dynamic_slice_in_dim(pair, lax.axis_index("xh") * PART, PART, axis=1)
    own = lax.ppermute(own.reshape(SLICE, LANES), whole, same)
    gathered = lax.all_gather(pair.reshape(2 * SLICE, LANES), "z", axis=0, tiled=True)
    image, vra, vrb = call(
        image_kernel,
        [(ROWS * 96, LANES), (1024, LANES), (1024, LANES)],
        [],
        2 * 1024 * 512 * 192,
        blocks,
        gathered,
        own,
    )
    image = spread(image.reshape(ROWS, 96, LANES), "row").reshape(-1, LANES)
    block, mine, vca, vcb = call(
        slice_kernel,
        [(BLOCK, LANES), (ROWS, SLICE, LANES), (512, LANES), (512, LANES)],
        [(SLICE, LANES)],
        2 * 512 * 192 * 96,
        image,
    )
    y_cols = spread(mine, "row").reshape(-1, LANES)
    block = lax.all_gather(block, "z")
    (block,) = call(turn_kernel, [(2 * ROWS, BLOCK, LANES)], [], 0, block)
    y_rows = spread(block, ("row", "xh")).reshape(-1, LANES)
    (out,) = call(
        update_kernel,
        [(4096, LANES)],
        [(192, 1024), (192, 512)],
        2 * 1024 * 512 * 384,
        blocks,
        vra,
        vrb,
        vca,
        vcb,
        y_cols,
        y_rows,
        factors,
    )
    return out.reshape(matrix.shape)


def solution(mesh):
    finer = Mesh(mesh.devices.reshape(ROWS, XS, ZS), ("row", "xh", "z"))
    cols = ("xh", "z")
    placed = (P(None, "row", None, None, cols, None), P(None, None, "row", cols, None), P())
    return jax.shard_map(
        shards,
        mesh=finer,
        in_specs=placed,
        out_specs=placed[0],
        check_vma=False,
    )
```

```python
import jax
import jax.numpy as jnp
from jax import lax
from jax.experimental import pallas as pl
from jax.experimental.pallas import tpu as pltpu
from jax.sharding import Mesh
from jax.sharding import PartitionSpec as P

ROWS = 16
ZS = 16
XS = 2
W = 96
LANES = 128
SLICE = 48
PART = 24
BLOCK = 72


def dot(a, b, ca=1, cb=0):
    return lax.dot_general(
        a,
        b,
        (((ca,), (cb,)), ((), ())),
        precision=lax.Precision.HIGHEST,
        preferred_element_type=jnp.float32,
    )


def parts(x):
    high = x.astype(jnp.bfloat16)
    return high, (x - high.astype(jnp.float32)).astype(jnp.bfloat16)


def left_parts(x):
    high, low = parts(x)
    return jnp.concatenate([high, low, high], axis=1)


def right_parts(x):
    high, low = parts(x)
    return jnp.concatenate([high, high, low], axis=0)


def plain(a, b):
    return lax.dot_general(
        a, b, (((1,), (0,)), ((), ())), preferred_element_type=jnp.float32
    )


HBM = pl.BlockSpec(memory_space=pltpu.HBM)
VMEM = pl.BlockSpec(memory_space=pltpu.VMEM)


def call(kernel, outs, scratch, flops, *args, in_hbm=(), out_hbm=()):
    shapes = [jax.ShapeDtypeStruct(s, jnp.float32) for s in outs]
    moved = sum(x.size for x in list(args) + shapes) * 4
    return pl.pallas_call(
        kernel,
        out_shape=shapes,
        in_specs=[HBM if k in in_hbm else VMEM for k in range(len(args))],
        out_specs=[HBM if k in out_hbm else VMEM for k in range(len(outs))],
        scratch_shapes=[pltpu.VMEM(s, jnp.float32) if isinstance(s, tuple) else s for s in scratch],
        compiler_params=pltpu.CompilerParams(vmem_limit_bytes=40 * 1024 * 1024),
        cost_estimate=pl.CostEstimate(flops=flops, bytes_accessed=moved, transcendentals=0),
    )(*args)


def pack_kernel(v_ref, out_ref):
    first = [jnp.concatenate([v_ref[0, i], v_ref[1, i][:, :32]], axis=1) for i in range(8)]
    rest = [v_ref[1, i][:, 32:] for i in range(8)]
    parts = []
    for h in range(2):
        parts += [first[2 * j + h] for j in range(4)]
        parts += [
            jnp.concatenate([rest[2 * j + h], rest[2 * j + 4 + h]], axis=1) for j in range(2)
        ]
    out_ref[...] = jnp.concatenate(parts, axis=0)


def fetch(hbm_ref, a_ref, sem, pieces):
    rows = a_ref.shape[0] // pieces
    copies = []
    for k in range(pieces):
        at = pl.ds(k * rows, rows)
        copies.append(pltpu.make_async_copy(hbm_ref.at[at, :], a_ref.at[at, :], sem.at[k]))
        copies[-1].start()
    return copies


def image_kernel(hbm_ref, g_ref, own_ref, send_ref, va_ref, vb_ref, a_ref, sem):
    copies = fetch(hbm_ref, a_ref, sem, 4)
    for x in range(XS):
        for j in range(4):
            for h in range(2):
                for r in range(4):
                    to = pl.ds((2 * j + h) * 128 + x * 64 + r, 16, stride=4)
                    va_ref[to, :] = g_ref[
                        pl.ds(x * SLICE + h * PART + j * 4 + r, 16, stride=2 * SLICE), :
                    ]
        for j in range(2):
            for h in range(2):
                for r in range(4):
                    both = g_ref[
                        pl.ds(x * SLICE + h * PART + 16 + j * 4 + r, 16, stride=2 * SLICE), :
                    ]
                    at = (2 * j + h) * 128 + x * 64 + r
                    vb_ref[pl.ds(at, 16, stride=4), :] = both
                    vb_ref[pl.ds(at + 512, 16, stride=4), :] = pltpu.roll(both, 64, 1)
    v = left_parts(jnp.concatenate([va_ref[...], vb_ref[:, :64]], axis=1).T)
    for copy in copies:
        copy.wait()
    for half in range(2):
        tiles = [a_ref[pl.ds(2 * half + t, 1024, stride=4), :] for t in range(2)]
        q = plain(v, right_parts(jnp.concatenate(tiles, axis=1)))
        for t in range(2):
            j = 2 * half + t
            for kk in range(12):
                send_ref[pl.ds(kk * 4 + j, 16, stride=2 * SLICE), :] = q[
                    kk * 16 : kk * 16 + 16, t * 128 : t * 128 + 128
                ]
    own = own_ref[...]
    for k in range(ROWS):
        send_ref[k * 96 + 48 : k * 96 + 96, :] = own


def slice_kernel(r_ref, block_ref, y_ref, va_ref, vb_ref, sum_ref):
    me = lax.axis_index("row")
    total = r_ref[0:48, :]
    for k in range(1, ROWS):
        total = total + r_ref[k * 96 : k * 96 + 48, :]
    sum_ref[...] = total
    for x in range(XS):
        for j in range(4):
            for r in range(4):
                va_ref[pl.ds(j * 128 + x * 64 + r, 16, stride=4), :] = r_ref[
                    pl.ds(48 + x * 24 + j * 4 + r, 16, stride=96), :
                ]
        for j in range(2):
            for r in range(4):
                both = r_ref[pl.ds(64 + x * 24 + j * 4 + r, 16, stride=96), :]
                vb_ref[pl.ds(j * 128 + x * 64 + r, 16, stride=4), :] = both
                vb_ref[pl.ds((j + 2) * 128 + x * 64 + r, 16, stride=4), :] = pltpu.roll(both, 64, 1)
    v = jnp.concatenate([va_ref[...], vb_ref[:, :64]], axis=1)
    y = jnp.concatenate([sum_ref[pl.ds(j, 12, stride=4), :] for j in range(4)], axis=1)
    ht = dot(y, v)
    gram = dot(v[:, :W], v[:, W:], 0, 0)
    at = lax.broadcasted_iota(jnp.int32, (8, W), 0) * 16 + me
    pick = jnp.where(at == lax.broadcasted_iota(jnp.int32, (8, W), 1), 1.0, 0.0)
    mine = dot(pick, gram)
    low = jnp.concatenate([ht[0:6, 128:], ht[6:12, 128:]], axis=1)
    mine = jnp.concatenate([mine[0:6], jnp.zeros((6, 32), jnp.float32)], axis=1)
    tail = jnp.concatenate([ht[:, :128], low, mine], axis=0)
    block_ref[0:48, :] = total
    block_ref[48:72, :] = tail
    for k in range(ROWS):
        y_ref[k] = total


def turn_kernel(r_ref, out_ref):
    tail = r_ref[0, 48:72, :]
    for k in range(1, ZS):
        tail = tail + r_ref[k, 48:72, :]
    for k in range(ROWS):
        for x in range(XS):
            out_ref[2 * k + x, 0:48, :] = r_ref[k, 0:48, :]
            out_ref[2 * k + x, 48:72, :] = tail


def update_kernel(
    hbm_ref, vra_ref, vrb_ref, vca_ref, vcb_ref, y_ref, r_ref, t_ref, to_ref,
    a_ref, out_ref, yr_ref, yc_ref, left_ref, sem, out_sem,
):
    copies = fetch(hbm_ref, a_ref, sem, 4)

    def both(start):
        here = r_ref[pl.ds(start, 16, stride=2 * BLOCK), :]
        return here + r_ref[pl.ds(start + BLOCK, 16, stride=2 * BLOCK), :]

    def mul(a, b):
        return plain(left_parts(a), right_parts(b))

    wide = [both(48 + k) for k in range(12)]
    low = [both(60 + k) for k in range(6)]
    h11 = jnp.concatenate(wide[:6], axis=0)[:, :W]
    h_a = jnp.concatenate(wide, axis=0)
    h_b = jnp.concatenate([x[:, :64] for x in low] + [x[:, 64:] for x in low], axis=0)
    ht = jnp.concatenate([h_a[:, W:], h_b], axis=1)
    h12 = ht[:W]
    h22 = ht[W:]
    g = jnp.concatenate([both(66 + k) for k in range(6)], axis=0)[:, :W]
    t1 = t_ref[0]
    t2 = t_ref[1]
    t1t = t1.T
    tg = mul(t1, g)
    inner = h12 - 0.5 * mul(h11, tg)
    shift1 = 0.5 * mul(t1t, mul(h11, t1))
    crossed = mul(t1t, inner)
    fold = mul(tg.T, inner)
    second = h22 - fold - fold.T
    shift2 = 0.5 * mul(t2.T, mul(second, t2))
    corner = mul(crossed, t2) - mul(shift1, mul(g, t2))
    none = jnp.zeros((W, W), jnp.float32)
    left = jnp.concatenate(
        [
            jnp.concatenate([t1, -mul(tg, t2)], axis=1),
            jnp.concatenate([none, t2], axis=1),
        ],
        axis=0,
    )
    sym = jnp.concatenate(
        [
            jnp.concatenate([shift1 + shift1.T, corner], axis=1),
            jnp.concatenate([corner.T, shift2 + shift2.T], axis=1),
        ],
        axis=0,
    )
    for k in range(12):
        for j in range(4):
            for x in range(XS):
                i = 2 * j + x
                yr_ref[k * 16 : k * 16 + 16, i * 128 : i * 128 + 128] = r_ref[
                    pl.ds(x * BLOCK + k * 4 + j, 16, stride=2 * BLOCK), :
                ]
            yc_ref[k * 16 : k * 16 + 16, j * 128 : j * 128 + 128] = y_ref[
                pl.ds(k * 4 + j, 16, stride=SLICE), :
            ]
    for i in range(4):
        at = slice(i * 256, i * 256 + 256)
        rows = jnp.concatenate(
            [vra_ref[at, :], vrb_ref[at, :64], yr_ref[:, at].T], axis=1
        )
        left_ref[at, :] = left_parts(rows)
    vc = jnp.concatenate([vca_ref[...], vcb_ref[:, :64]], axis=1).T
    m1 = mul(left.T, yc_ref[...]) - mul(sym, vc)
    m2 = mul(left, vc)
    right = right_parts(jnp.concatenate([m1, m2], axis=0))
    for copy in copies:
        copy.wait()
    outs = []
    for i in range(4):
        at = i * 256
        change = plain(left_ref[at : at + 256, :], right)
        for j in range(4):
            where = pl.ds(at * 4 + j, 256, stride=4)
            out_ref[where, :] = a_ref[where, :] - change[:, j * 128 : j * 128 + 128]
        part = pl.ds(at * 4, 1024)
        outs.append(pltpu.make_async_copy(out_ref.at[part, :], to_ref.at[part, :], out_sem.at[i]))
        outs[-1].start()
    for copy in outs:
        copy.wait()


def spread(array, axes):
    return lax.all_to_all(array, axes, split_axis=0, concat_axis=0, tiled=True)


def shards(matrix, vectors, factors):
    blocks = pltpu.with_memory_space_constraint(matrix.reshape(-1, LANES), pltpu.HBM)
    every = [(p, x, z) for p in range(ROWS) for x in range(XS) for z in range(ZS)]
    number = {at: k for k, at in enumerate(every)}
    same = [(number[p, x, z], number[z, x, p]) for p, x, z in every]
    whole = ("row", "xh", "z")

    (packed,) = call(pack_kernel, [(SLICE, LANES)], [], 0, vectors.reshape(2, 8, 4, W))
    pair = lax.all_gather(packed, "xh")
    own = lax.dynamic_slice_in_dim(pair, lax.axis_index("xh") * PART, PART, axis=1)
    own = lax.ppermute(own.reshape(SLICE, LANES), whole, same)
    gathered = lax.all_gather(pair.reshape(2 * SLICE, LANES), "z", axis=0, tiled=True)
    image, vra, vrb = call(
        image_kernel,
        [(ROWS * 96, LANES), (1024, LANES), (1024, LANES)],
        [(4096, LANES), pltpu.SemaphoreType.DMA((4,))],
        2 * 1024 * 512 * 192,
        blocks,
        gathered,
        own,
        in_hbm=(0,),
    )
    image = spread(image.reshape(ROWS, 96, LANES), "row").reshape(-1, LANES)
    block, mine, vca, vcb = call(
        slice_kernel,
        [(BLOCK, LANES), (ROWS, SLICE, LANES), (512, LANES), (512, LANES)],
        [(SLICE, LANES)],
        2 * 512 * 192 * 96,
        image,
    )
    y_cols = spread(mine, "row").reshape(-1, LANES)
    block = lax.all_gather(block, "z")
    (block,) = call(turn_kernel, [(2 * ROWS, BLOCK, LANES)], [], 0, block)
    y_rows = spread(block, ("row", "xh")).reshape(-1, LANES)
    (out,) = call(
        update_kernel,
        [(4096, LANES)],
        [
            (4096, LANES),
            (4096, LANES),
            (192, 1024),
            (192, 512),
            pltpu.VMEM((1024, 1152), jnp.bfloat16),
            pltpu.SemaphoreType.DMA((4,)),
            pltpu.SemaphoreType.DMA((4,)),
        ],
        2 * 1024 * 512 * 384,
        blocks,
        vra,
        vrb,
        vca,
        vcb,
        y_cols,
        y_rows,
        factors,
        in_hbm=(0,),
        out_hbm=(0,),
    )
    return out.reshape(matrix.shape)


def solution(mesh):
    finer = Mesh(mesh.devices.reshape(ROWS, XS, ZS), ("row", "xh", "z"))
    cols = ("xh", "z")
    placed = (P(None, "row", None, None, cols, None), P(None, None, "row", cols, None), P())
    return jax.shard_map(
        shards,
        mesh=finer,
        in_specs=placed,
        out_specs=placed[0],
        check_vma=False,
    )
```

```python
import jax
import jax.numpy as jnp
from jax import lax
from jax.experimental import pallas as pl
from jax.experimental.pallas import tpu as pltpu
from jax.sharding import Mesh
from jax.sharding import PartitionSpec as P

ROWS = 16
ZS = 16
XS = 2
W = 96
LANES = 128
SLICE = 48
PART = 24
BLOCK = 64
MINE = 56
SEND = 104


def dot(a, b, ca=1, cb=0):
    return lax.dot_general(
        a,
        b,
        (((ca,), (cb,)), ((), ())),
        precision=lax.Precision.HIGHEST,
        preferred_element_type=jnp.float32,
    )


def parts(x):
    high = x.astype(jnp.bfloat16)
    return high, (x - high.astype(jnp.float32)).astype(jnp.bfloat16)


def left_parts(x):
    high, low = parts(x)
    return jnp.concatenate([high, low, high], axis=1)


def right_parts(x):
    high, low = parts(x)
    return jnp.concatenate([high, high, low], axis=0)


def plain(a, b):
    return lax.dot_general(
        a, b, (((1,), (0,)), ((), ())), preferred_element_type=jnp.float32
    )


HBM = pl.BlockSpec(memory_space=pltpu.HBM)
VMEM = pl.BlockSpec(memory_space=pltpu.VMEM)


def call(kernel, outs, scratch, flops, *args, in_hbm=(), out_hbm=()):
    shapes = [jax.ShapeDtypeStruct(s, jnp.float32) for s in outs]
    moved = sum(x.size for x in list(args) + shapes) * 4
    return pl.pallas_call(
        kernel,
        out_shape=shapes,
        in_specs=[HBM if k in in_hbm else VMEM for k in range(len(args))],
        out_specs=[HBM if k in out_hbm else VMEM for k in range(len(outs))],
        scratch_shapes=[pltpu.VMEM(s, jnp.float32) if isinstance(s, tuple) else s for s in scratch],
        compiler_params=pltpu.CompilerParams(vmem_limit_bytes=40 * 1024 * 1024),
        cost_estimate=pl.CostEstimate(flops=flops, bytes_accessed=moved, transcendentals=0),
    )(*args)


def pack_kernel(v_ref, out_ref):
    first = [jnp.concatenate([v_ref[0, i], v_ref[1, i][:, :32]], axis=1) for i in range(8)]
    rest = [v_ref[1, i][:, 32:] for i in range(8)]
    parts = []
    for h in range(2):
        parts += [first[2 * j + h] for j in range(4)]
        parts += [
            jnp.concatenate([rest[2 * j + h], rest[2 * j + 4 + h]], axis=1) for j in range(2)
        ]
    out_ref[...] = jnp.concatenate(parts, axis=0)


def fetch(hbm_ref, a_ref, sem, pieces):
    rows = a_ref.shape[0] // pieces
    copies = []
    for k in range(pieces):
        at = pl.ds(k * rows, rows)
        copies.append(pltpu.make_async_copy(hbm_ref.at[at, :], a_ref.at[at, :], sem.at[k]))
        copies[-1].start()
    return copies


def image_kernel(hbm_ref, g_ref, own_ref, send_ref, va_ref, vb_ref, a_ref, sem):
    copies = fetch(hbm_ref, a_ref, sem, 8)
    for x in range(XS):
        for j in range(4):
            for h in range(2):
                for r in range(4):
                    to = pl.ds((2 * j + h) * 128 + x * 64 + r, 16, stride=4)
                    va_ref[to, :] = g_ref[
                        pl.ds(x * SLICE + h * PART + j * 4 + r, 16, stride=2 * SLICE), :
                    ]
        for j in range(2):
            for h in range(2):
                for r in range(4):
                    both = g_ref[
                        pl.ds(x * SLICE + h * PART + 16 + j * 4 + r, 16, stride=2 * SLICE), :
                    ]
                    at = (2 * j + h) * 128 + x * 64 + r
                    vb_ref[pl.ds(at, 16, stride=4), :] = both
                    vb_ref[pl.ds(at + 512, 16, stride=4), :] = pltpu.roll(both, 64, 1)
    q = 0.0
    gram = 0.0
    for c in range(4):
        at = slice(c * 256, c * 256 + 256)
        v = jnp.concatenate([va_ref[at, :], vb_ref[at, :64]], axis=1)
        left = left_parts(v.T)
        gram = gram + plain(left[:W], right_parts(v[:, W:]))
        copies[2 * c].wait()
        copies[2 * c + 1].wait()
        tiles = [a_ref[pl.ds(c * 1024 + j, 256, stride=4), :] for j in range(4)]
        q = q + plain(left, right_parts(jnp.concatenate(tiles, axis=1)))
    for j in range(4):
        for kk in range(12):
            send_ref[pl.ds(kk * 4 + j, 16, stride=SEND), :] = q[
                kk * 16 : kk * 16 + 16, j * 128 : j * 128 + 128
            ]
    gram = jnp.concatenate([gram, jnp.zeros((W, 32), jnp.float32)], axis=1)
    for k in range(8):
        rows = gram[k * 16 : k * 16 + 16] if k < 6 else jnp.zeros((16, LANES), jnp.float32)
        send_ref[pl.ds(SLICE + k, 16, stride=SEND), :] = rows
    own = own_ref[...]
    for k in range(ROWS):
        send_ref[k * SEND + MINE : k * SEND + SEND, :] = own


def slice_kernel(r_ref, block_ref, y_ref, va_ref, vb_ref, sum_ref):
    total = r_ref[0:MINE, :]
    for k in range(1, ROWS):
        total = total + r_ref[k * SEND : k * SEND + MINE, :]
    sum_ref[...] = total
    for x in range(XS):
        for j in range(4):
            for r in range(4):
                va_ref[pl.ds(j * 128 + x * 64 + r, 16, stride=4), :] = r_ref[
                    pl.ds(MINE + x * 24 + j * 4 + r, 16, stride=SEND), :
                ]
        for j in range(2):
            for r in range(4):
                both = r_ref[pl.ds(MINE + 16 + x * 24 + j * 4 + r, 16, stride=SEND), :]
                vb_ref[pl.ds(j * 128 + x * 64 + r, 16, stride=4), :] = both
                vb_ref[pl.ds((j + 2) * 128 + x * 64 + r, 16, stride=4), :] = pltpu.roll(both, 64, 1)
    v = jnp.concatenate([va_ref[...], vb_ref[:, :64]], axis=1)
    y = jnp.concatenate([sum_ref[pl.ds(j, 12, stride=4), :] for j in range(4)], axis=1)
    ht = dot(y, v)
    low = jnp.concatenate([ht[0:6, LANES:], ht[6:12, W : W + 64]], axis=1)
    end = ht[6:12, W + 64 :]
    none = jnp.zeros((1, 32), jnp.float32)
    ends = [
        jnp.concatenate([end[k : k + 1], end[k + 1 : k + 2], end[k + 2 : k + 3], none], axis=1)
        for k in (0, 3)
    ]
    block_ref[0:48, :] = total[:SLICE]
    block_ref[48:64, :] = jnp.concatenate(
        [ht[0:6, :LANES], low] + ends + [jnp.zeros((2, LANES), jnp.float32)], axis=0
    )
    for k in range(ROWS):
        y_ref[k] = total


def turn_kernel(r_ref, out_ref):
    tail = r_ref[0, 48:BLOCK, :]
    for k in range(1, ZS):
        tail = tail + r_ref[k, 48:BLOCK, :]
    for k in range(ROWS):
        for x in range(XS):
            out_ref[2 * k + x, 0:48, :] = r_ref[k, 0:48, :]
            out_ref[2 * k + x, 48:BLOCK, :] = tail


def update_kernel(
    hbm_ref, vra_ref, vrb_ref, vca_ref, vcb_ref, y_ref, r_ref, t_ref, to_ref,
    a_ref, out_ref, yr_ref, yc_ref, left_ref, sem, out_sem,
):
    copies = fetch(hbm_ref, a_ref, sem, 4)

    def both(start):
        here = r_ref[pl.ds(start, 16, stride=2 * BLOCK), :]
        return here + r_ref[pl.ds(start + BLOCK, 16, stride=2 * BLOCK), :]

    def mul(a, b):
        return plain(left_parts(a), right_parts(b))

    wide = jnp.concatenate([both(48 + k) for k in range(6)], axis=0)
    low = jnp.concatenate([both(54 + k) for k in range(6)], axis=0)
    ends = [both(60 + k) for k in range(2)]
    end = jnp.concatenate(
        [ends[k // 3][:, k % 3 * 32 : k % 3 * 32 + 32] for k in range(6)], axis=0
    )
    h11 = wide[:, :W]
    h12 = jnp.concatenate([wide[:, W:], low[:, :64]], axis=1)
    h22 = jnp.concatenate([low[:, 64:], end], axis=1)
    g = [y_ref[pl.ds(SLICE + k, 16, stride=MINE), :] for k in range(6)]
    g = jnp.concatenate(g, axis=0)[:, :W]
    t1 = t_ref[0]
    t2 = t_ref[1]
    t1t = t1.T
    tg = mul(t1, g)
    inner = h12 - 0.5 * mul(h11, tg)
    shift1 = 0.5 * mul(t1t, mul(h11, t1))
    crossed = mul(t1t, inner)
    fold = mul(tg.T, inner)
    second = h22 - fold - fold.T
    shift2 = 0.5 * mul(t2.T, mul(second, t2))
    corner = mul(crossed, t2) - mul(shift1, mul(g, t2))
    none = jnp.zeros((W, W), jnp.float32)
    left = jnp.concatenate(
        [
            jnp.concatenate([t1, -mul(tg, t2)], axis=1),
            jnp.concatenate([none, t2], axis=1),
        ],
        axis=0,
    )
    sym = jnp.concatenate(
        [
            jnp.concatenate([shift1 + shift1.T, corner], axis=1),
            jnp.concatenate([corner.T, shift2 + shift2.T], axis=1),
        ],
        axis=0,
    )
    for k in range(12):
        for j in range(4):
            for x in range(XS):
                i = 2 * j + x
                yr_ref[k * 16 : k * 16 + 16, i * 128 : i * 128 + 128] = r_ref[
                    pl.ds(x * BLOCK + k * 4 + j, 16, stride=2 * BLOCK), :
                ]
            yc_ref[k * 16 : k * 16 + 16, j * 128 : j * 128 + 128] = y_ref[
                pl.ds(k * 4 + j, 16, stride=MINE), :
            ]
    for i in range(4):
        at = slice(i * 256, i * 256 + 256)
        rows = jnp.concatenate(
            [vra_ref[at, :], vrb_ref[at, :64], yr_ref[:, at].T], axis=1
        )
        left_ref[at, :] = left_parts(rows)
    vc = jnp.concatenate([vca_ref[...], vcb_ref[:, :64]], axis=1).T
    m1 = mul(left.T, yc_ref[...]) - mul(sym, vc)
    m2 = mul(left, vc)
    right = right_parts(jnp.concatenate([m1, m2], axis=0))
    for copy in copies:
        copy.wait()
    outs = []
    for i in range(4):
        at = i * 256
        change = plain(left_ref[at : at + 256, :], right)
        for j in range(4):
            where = pl.ds(at * 4 + j, 256, stride=4)
            out_ref[where, :] = a_ref[where, :] - change[:, j * 128 : j * 128 + 128]
        part = pl.ds(at * 4, 1024)
        outs.append(pltpu.make_async_copy(out_ref.at[part, :], to_ref.at[part, :], out_sem.at[i]))
        outs[-1].start()
    for copy in outs:
        copy.wait()


def spread(array, axes):
    return lax.all_to_all(array, axes, split_axis=0, concat_axis=0, tiled=True)


def shards(matrix, vectors, factors):
    blocks = pltpu.with_memory_space_constraint(matrix.reshape(-1, LANES), pltpu.HBM)
    every = [(p, x, z) for p in range(ROWS) for x in range(XS) for z in range(ZS)]
    number = {at: k for k, at in enumerate(every)}
    same = [(number[p, x, z], number[z, x, p]) for p, x, z in every]
    whole = ("row", "xh", "z")

    (packed,) = call(pack_kernel, [(SLICE, LANES)], [], 0, vectors.reshape(2, 8, 4, W))
    pair = lax.all_gather(packed, "xh")
    own = lax.dynamic_slice_in_dim(pair, lax.axis_index("xh") * PART, PART, axis=1)
    own = lax.ppermute(own.reshape(SLICE, LANES), whole, same)
    gathered = lax.all_gather(pair.reshape(2 * SLICE, LANES), "z", axis=0, tiled=True)
    image, vra, vrb = call(
        image_kernel,
        [(ROWS * SEND, LANES), (1024, LANES), (1024, LANES)],
        [(4096, LANES), pltpu.SemaphoreType.DMA((8,))],
        2 * 1024 * 512 * 192,
        blocks,
        gathered,
        own,
        in_hbm=(0,),
    )
    image = spread(image.reshape(ROWS, SEND, LANES), "row").reshape(-1, LANES)
    block, mine, vca, vcb = call(
        slice_kernel,
        [(BLOCK, LANES), (ROWS, MINE, LANES), (512, LANES), (512, LANES)],
        [(MINE, LANES)],
        2 * 512 * 192 * 96,
        image,
    )
    y_cols = spread(mine, "row").reshape(-1, LANES)
    block = lax.all_gather(block, "z")
    (block,) = call(turn_kernel, [(2 * ROWS, BLOCK, LANES)], [], 0, block)
    y_rows = spread(block, ("row", "xh")).reshape(-1, LANES)
    (out,) = call(
        update_kernel,
        [(4096, LANES)],
        [
            (4096, LANES),
            (4096, LANES),
            (192, 1024),
            (192, 512),
            pltpu.VMEM((1024, 1152), jnp.bfloat16),
            pltpu.SemaphoreType.DMA((4,)),
            pltpu.SemaphoreType.DMA((4,)),
        ],
        2 * 1024 * 512 * 384,
        blocks,
        vra,
        vrb,
        vca,
        vcb,
        y_cols,
        y_rows,
        factors,
        in_hbm=(0,),
        out_hbm=(0,),
    )
    return out.reshape(matrix.shape)


def solution(mesh):
    finer = Mesh(mesh.devices.reshape(ROWS, XS, ZS), ("row", "xh", "z"))
    cols = ("xh", "z")
    placed = (P(None, "row", None, None, cols, None), P(None, None, "row", cols, None), P())
    return jax.shard_map(
        shards,
        mesh=finer,
        in_specs=placed,
        out_specs=placed[0],
        check_vma=False,
    )
```

```python
import jax
import jax.numpy as jnp
from jax import lax
from jax.experimental import pallas as pl
from jax.experimental.pallas import tpu as pltpu
from jax.sharding import Mesh
from jax.sharding import PartitionSpec as P

ROWS = 16
ZS = 16
XS = 2
W = 96
LANES = 128
SLICE = 48
PART = 24
BLOCK = 64
MINE = 56
SEND = 104


def dot(a, b, ca=1, cb=0):
    return lax.dot_general(
        a,
        b,
        (((ca,), (cb,)), ((), ())),
        precision=lax.Precision.HIGHEST,
        preferred_element_type=jnp.float32,
    )


def parts(x):
    high = x.astype(jnp.bfloat16)
    return high, (x - high.astype(jnp.float32)).astype(jnp.bfloat16)


def left_parts(x):
    high, low = parts(x)
    return jnp.concatenate([high, low, high], axis=1)


def right_parts(x):
    high, low = parts(x)
    return jnp.concatenate([high, high, low], axis=0)


def plain(a, b):
    return lax.dot_general(
        a, b, (((1,), (0,)), ((), ())), preferred_element_type=jnp.float32
    )


def times(a, b):
    return plain(a[0], b[0]) + plain(a[1], b[0]) + plain(a[0], b[1])


def mul(a, b):
    return times(parts(a), parts(b))


HBM = pl.BlockSpec(memory_space=pltpu.HBM)
VMEM = pl.BlockSpec(memory_space=pltpu.VMEM)


def call(kernel, outs, scratch, flops, *args, in_hbm=(), out_hbm=()):
    shapes = [
        jax.ShapeDtypeStruct(s, jnp.float32) if isinstance(s[0], int) else jax.ShapeDtypeStruct(*s)
        for s in outs
    ]
    moved = sum(x.size for x in list(args) + shapes) * 4
    shapes = [
        pltpu.HBM(x.shape, x.dtype) if k in out_hbm else x for k, x in enumerate(shapes)
    ]
    return list(pl.pallas_call(
        kernel,
        out_shape=shapes,
        in_specs=[HBM if k in in_hbm else VMEM for k in range(len(args))],
        out_specs=[HBM if k in out_hbm else VMEM for k in range(len(outs))],
        scratch_shapes=[pltpu.VMEM(s, jnp.float32) if isinstance(s, tuple) else s for s in scratch],
        compiler_params=pltpu.CompilerParams(vmem_limit_bytes=40 * 1024 * 1024),
        cost_estimate=pl.CostEstimate(flops=flops, bytes_accessed=moved, transcendentals=0),
    )(*args))


def pack_kernel(v_ref, out_ref):
    first = [jnp.concatenate([v_ref[0, i], v_ref[1, i][:, :32]], axis=1) for i in range(8)]
    rest = [v_ref[1, i][:, 32:] for i in range(8)]
    parts = []
    for h in range(2):
        parts += [first[2 * j + h] for j in range(4)]
        parts += [
            jnp.concatenate([rest[2 * j + h], rest[2 * j + 4 + h]], axis=1) for j in range(2)
        ]
    out_ref[...] = jnp.concatenate(parts, axis=0)


def fetch(hbm_ref, a_ref, sem, pieces):
    rows = a_ref.shape[0] // pieces
    copies = []
    for k in range(pieces):
        at = pl.ds(k * rows, rows)
        copies.append(pltpu.make_async_copy(hbm_ref.at[at, :], a_ref.at[at, :], sem.at[k]))
        copies[-1].start()
    return copies


def move(sources, targets, sem):
    copies = [
        pltpu.make_async_copy(source, target, sem.at[k])
        for k, (source, target) in enumerate(zip(sources, targets))
    ]
    for copy in copies:
        copy.start()
    return copies


def image_kernel(hbm_ref, g_ref, own_ref, send_ref, va_ref, vb_ref, a_ref, sem):
    copies = fetch(hbm_ref, a_ref, sem, 8)
    for x in range(XS):
        for j in range(4):
            for h in range(2):
                for r in range(4):
                    to = pl.ds((2 * j + h) * 128 + x * 64 + r, 16, stride=4)
                    va_ref[to, :] = g_ref[
                        pl.ds(x * SLICE + h * PART + j * 4 + r, 16, stride=2 * SLICE), :
                    ]
        for j in range(2):
            for h in range(2):
                for r in range(4):
                    both = g_ref[
                        pl.ds(x * SLICE + h * PART + 16 + j * 4 + r, 16, stride=2 * SLICE), :
                    ]
                    at = (2 * j + h) * 128 + x * 64 + r
                    vb_ref[pl.ds(at, 16, stride=4), :] = both
                    vb_ref[pl.ds(at + 512, 16, stride=4), :] = pltpu.roll(both, 64, 1)
    q = 0.0
    gram = 0.0
    for c in range(4):
        at = slice(c * 256, c * 256 + 256)
        v = jnp.concatenate([va_ref[at, :], vb_ref[at, :64]], axis=1)
        left = left_parts(v.T)
        gram = gram + plain(left[:W], right_parts(v[:, W:]))
        copies[2 * c].wait()
        copies[2 * c + 1].wait()
        tiles = [a_ref[pl.ds(c * 1024 + j, 256, stride=4), :] for j in range(4)]
        q = q + plain(left, right_parts(jnp.concatenate(tiles, axis=1)))
    for j in range(4):
        for kk in range(12):
            send_ref[pl.ds(kk * 4 + j, 16, stride=SEND), :] = q[
                kk * 16 : kk * 16 + 16, j * 128 : j * 128 + 128
            ]
    gram = jnp.concatenate([gram, jnp.zeros((W, 32), jnp.float32)], axis=1)
    for k in range(8):
        rows = gram[k * 16 : k * 16 + 16] if k < 6 else jnp.zeros((16, LANES), jnp.float32)
        send_ref[pl.ds(SLICE + k, 16, stride=SEND), :] = rows
    own = own_ref[...]
    for k in range(ROWS):
        send_ref[k * SEND + MINE : k * SEND + SEND, :] = own


def slice_kernel(r_ref, block_ref, y_ref, to_a, to_b, sum_ref, va_ref, vb_ref, sem):
    total = r_ref[0:MINE, :]
    for k in range(1, ROWS):
        total = total + r_ref[k * SEND : k * SEND + MINE, :]
    sum_ref[...] = total
    for x in range(XS):
        for j in range(4):
            for r in range(4):
                va_ref[pl.ds(j * 128 + x * 64 + r, 16, stride=4), :] = r_ref[
                    pl.ds(MINE + x * 24 + j * 4 + r, 16, stride=SEND), :
                ]
        for j in range(2):
            for r in range(4):
                both = r_ref[pl.ds(MINE + 16 + x * 24 + j * 4 + r, 16, stride=SEND), :]
                vb_ref[pl.ds(j * 128 + x * 64 + r, 16, stride=4), :] = both
                vb_ref[pl.ds((j + 2) * 128 + x * 64 + r, 16, stride=4), :] = pltpu.roll(both, 64, 1)
    copies = move((va_ref, vb_ref), (to_a, to_b), sem)
    v = jnp.concatenate([va_ref[...], vb_ref[:, :64]], axis=1)
    y = jnp.concatenate([sum_ref[pl.ds(j, 12, stride=4), :] for j in range(4)], axis=1)
    ht = dot(y, v)
    low = jnp.concatenate([ht[0:6, LANES:], ht[6:12, W : W + 64]], axis=1)
    end = ht[6:12, W + 64 :]
    none = jnp.zeros((1, 32), jnp.float32)
    ends = [
        jnp.concatenate([end[k : k + 1], end[k + 1 : k + 2], end[k + 2 : k + 3], none], axis=1)
        for k in (0, 3)
    ]
    block_ref[0:48, :] = total[:SLICE]
    block_ref[48:64, :] = jnp.concatenate(
        [ht[0:6, :LANES], low] + ends + [jnp.zeros((2, LANES), jnp.float32)], axis=0
    )
    for k in range(ROWS):
        y_ref[k] = total
    for copy in copies:
        copy.wait()


def turn_kernel(r_ref, out_ref):
    tail = r_ref[0, 48:BLOCK, :]
    for k in range(1, ZS):
        tail = tail + r_ref[k, 48:BLOCK, :]
    for k in range(ROWS):
        for x in range(XS):
            out_ref[2 * k + x, 0:48, :] = r_ref[k, 0:48, :]
            out_ref[2 * k + x, 48:BLOCK, :] = tail


def ready_kernel(
    from_a, from_b, y_ref, t_ref, to_1, to_2, to_high, to_low, tg_ref, gt_ref,
    yc_ref, vca_ref, vcb_ref, m1_ref, m2_ref, high_ref, low_ref, sem, out_sem,
):
    copies = move((from_a, from_b), (vca_ref, vcb_ref), sem)
    for k in range(12):
        for j in range(4):
            yc_ref[k * 16 : k * 16 + 16, j * 128 : j * 128 + 128] = y_ref[
                pl.ds(k * 4 + j, 16, stride=MINE), :
            ]
    g = [y_ref[pl.ds(SLICE + k, 16, stride=MINE), :] for k in range(6)]
    g = jnp.concatenate(g, axis=0)[:, :W]
    t1 = t_ref[0]
    t2 = t_ref[1]
    tg = mul(t1, g)
    tg_ref[...] = tg
    gt_ref[...] = mul(g, t2)
    none = jnp.zeros((W, W), jnp.float32)
    left = jnp.concatenate(
        [
            jnp.concatenate([t1, -mul(tg, t2)], axis=1),
            jnp.concatenate([none, t2], axis=1),
        ],
        axis=0,
    )
    for copy in copies:
        copy.wait()
    vc = parts(jnp.concatenate([vca_ref[...], vcb_ref[:, :64]], axis=1).T)
    high_ref[...], low_ref[...] = vc
    m1_ref[...] = mul(left.T, yc_ref[...])
    m2_ref[...] = times(parts(left), vc)
    own = (m1_ref, m2_ref, high_ref, low_ref)
    for copy in move(own, (to_1, to_2, to_high, to_low), out_sem):
        copy.wait()


def update_kernel(
    hbm_ref, vra_ref, vrb_ref, from_1, from_2, from_high, from_low, tg_ref, gt_ref, r_ref, t_ref,
    to_ref, a_ref, out_ref, yr_ref, left_ref, m1_ref, m2_ref, high_ref, low_ref,
    sem, out_sem, in_sem,
):
    own = (high_ref, low_ref, m1_ref, m2_ref)
    given = move((from_high, from_low, from_1, from_2), own, in_sem)
    copies = fetch(hbm_ref, a_ref, sem, 4)

    def both(start):
        here = r_ref[pl.ds(start, 16, stride=2 * BLOCK), :]
        return here + r_ref[pl.ds(start + BLOCK, 16, stride=2 * BLOCK), :]

    wide = jnp.concatenate([both(48 + k) for k in range(6)], axis=0)
    low = jnp.concatenate([both(54 + k) for k in range(6)], axis=0)
    ends = [both(60 + k) for k in range(2)]
    end = jnp.concatenate(
        [ends[k // 3][:, k % 3 * 32 : k % 3 * 32 + 32] for k in range(6)], axis=0
    )
    h11 = wide[:, :W]
    h12 = jnp.concatenate([wide[:, W:], low[:, :64]], axis=1)
    h22 = jnp.concatenate([low[:, 64:], end], axis=1)
    t1 = t_ref[0]
    t2 = t_ref[1]
    t1t = t1.T
    tg = tg_ref[...]
    inner = h12 - 0.5 * mul(h11, tg)
    shift1 = 0.5 * mul(t1t, mul(h11, t1))
    crossed = mul(t1t, inner)
    fold = mul(tg.T, inner)
    second = h22 - fold - fold.T
    shift2 = 0.5 * mul(t2.T, mul(second, t2))
    corner = mul(crossed, t2) - mul(shift1, gt_ref[...])
    sym = jnp.concatenate(
        [
            jnp.concatenate([shift1 + shift1.T, corner], axis=1),
            jnp.concatenate([corner.T, shift2 + shift2.T], axis=1),
        ],
        axis=0,
    )
    for k in range(12):
        for j in range(4):
            for x in range(XS):
                i = 2 * j + x
                yr_ref[k * 16 : k * 16 + 16, i * 128 : i * 128 + 128] = r_ref[
                    pl.ds(x * BLOCK + k * 4 + j, 16, stride=2 * BLOCK), :
                ]
    for i in range(4):
        at = slice(i * 256, i * 256 + 256)
        y = yr_ref[:, at].T
        rows = jnp.concatenate(
            [vra_ref[at, :], y[:, :128], vrb_ref[at, :64], y[:, 128:]], axis=1
        )
        left_ref[at, :] = left_parts(rows)
    for copy in given:
        copy.wait()
    m1 = m1_ref[...] - times(parts(sym), (high_ref[...], low_ref[...]))
    m2 = m2_ref[...]
    right = right_parts(jnp.concatenate([m1[:128], m2[:128], m1[128:], m2[128:]], axis=0))
    for copy in copies:
        copy.wait()
    outs = []
    for i in range(4):
        at = i * 256
        change = plain(left_ref[at : at + 256, :], right)
        for j in range(4):
            where = pl.ds(at * 4 + j, 256, stride=4)
            out_ref[where, :] = a_ref[where, :] - change[:, j * 128 : j * 128 + 128]
        part = pl.ds(at * 4, 1024)
        outs.append(pltpu.make_async_copy(out_ref.at[part, :], to_ref.at[part, :], out_sem.at[i]))
        outs[-1].start()
    for copy in outs:
        copy.wait()


def spread(array, axes):
    return lax.all_to_all(array, axes, split_axis=0, concat_axis=0, tiled=True)


def shards(matrix, vectors, factors):
    blocks = pltpu.with_memory_space_constraint(matrix.reshape(-1, LANES), pltpu.HBM)
    every = [(p, x, z) for p in range(ROWS) for x in range(XS) for z in range(ZS)]
    number = {at: k for k, at in enumerate(every)}
    same = [(number[p, x, z], number[z, x, p]) for p, x, z in every]
    whole = ("row", "xh", "z")

    (packed,) = call(pack_kernel, [(SLICE, LANES)], [], 0, vectors.reshape(2, 8, 4, W))
    pair = lax.all_gather(packed, "xh")
    own = lax.dynamic_slice_in_dim(pair, lax.axis_index("xh") * PART, PART, axis=1)
    own = lax.ppermute(own.reshape(SLICE, LANES), whole, same)
    gathered = lax.all_gather(pair.reshape(2 * SLICE, LANES), "z", axis=0, tiled=True)
    image, vra, vrb = call(
        image_kernel,
        [(ROWS * SEND, LANES), (1024, LANES), (1024, LANES)],
        [(4096, LANES), pltpu.SemaphoreType.DMA((8,))],
        2 * 1024 * 512 * 192,
        blocks,
        gathered,
        own,
        in_hbm=(0,),
    )
    image = spread(image.reshape(ROWS, SEND, LANES), "row").reshape(-1, LANES)
    block, mine, vca, vcb = call(
        slice_kernel,
        [(BLOCK, LANES), (ROWS, MINE, LANES), (512, LANES), (512, LANES)],
        [(MINE, LANES), (512, LANES), (512, LANES), pltpu.SemaphoreType.DMA((2,))],
        2 * 512 * 192 * 96,
        image,
        out_hbm=(2, 3),
    )
    y_cols = spread(mine, "row").reshape(-1, LANES)
    block = lax.all_gather(block, "z")
    (block,) = call(turn_kernel, [(2 * ROWS, BLOCK, LANES)], [], 0, block)
    y_rows = spread(block, ("row", "xh")).reshape(-1, LANES)
    vca, vcb = (pltpu.with_memory_space_constraint(x, pltpu.HBM) for x in (vca, vcb))
    small = [(192, 512), (192, 512)]
    small += [((192, 512), jnp.bfloat16)] * 2 + [(W, W)] * 2
    half = pltpu.VMEM((192, 512), jnp.bfloat16)
    ready = call(
        ready_kernel,
        small,
        [
            (192, 512),
            (512, LANES),
            (512, LANES),
            (192, 512),
            (192, 512),
            half,
            half,
            pltpu.SemaphoreType.DMA((2,)),
            pltpu.SemaphoreType.DMA((4,)),
        ],
        12 * 192 * 192 * 512,
        vca,
        vcb,
        y_cols,
        factors,
        in_hbm=(0, 1),
        out_hbm=(0, 1, 2, 3),
    )
    ready[:4] = [pltpu.with_memory_space_constraint(x, pltpu.HBM) for x in ready[:4]]
    (out,) = call(
        update_kernel,
        [(4096, LANES)],
        [
            (4096, LANES),
            (4096, LANES),
            (192, 1024),
            pltpu.VMEM((1024, 1152), jnp.bfloat16),
            (192, 512),
            (192, 512),
            half,
            half,
            pltpu.SemaphoreType.DMA((4,)),
            pltpu.SemaphoreType.DMA((4,)),
            pltpu.SemaphoreType.DMA((4,)),
        ],
        2 * 1024 * 512 * 384,
        blocks,
        vra,
        vrb,
        *ready,
        y_rows,
        factors,
        in_hbm=(0, 3, 4, 5, 6),
        out_hbm=(0,),
    )
    return out.reshape(matrix.shape)


def solution(mesh):
    finer = Mesh(mesh.devices.reshape(ROWS, XS, ZS), ("row", "xh", "z"))
    cols = ("xh", "z")
    placed = (P(None, "row", None, None, cols, None), P(None, None, "row", cols, None), P())
    return jax.shard_map(
        shards,
        mesh=finer,
        in_specs=placed,
        out_specs=placed[0],
        check_vma=False,
    )
```

```python
import jax
import jax.numpy as jnp
from jax import lax
from jax.experimental import pallas as pl
from jax.experimental.pallas import tpu as pltpu
from jax.sharding import Mesh
from jax.sharding import PartitionSpec as P

ROWS = 16
ZS = 16
XS = 2
W = 96
LANES = 128
SLICE = 48
PART = 24
BLOCK = 64
MINE = 56
SEND = 104


def dot(a, b, ca=1, cb=0):
    return lax.dot_general(
        a,
        b,
        (((ca,), (cb,)), ((), ())),
        precision=lax.Precision.HIGHEST,
        preferred_element_type=jnp.float32,
    )


def parts(x):
    high = x.astype(jnp.bfloat16)
    return high, (x - high.astype(jnp.float32)).astype(jnp.bfloat16)


def left_parts(x):
    high, low = parts(x)
    return jnp.concatenate([high, low, high], axis=1)


def right_parts(x):
    high, low = parts(x)
    return jnp.concatenate([high, high, low], axis=0)


def plain(a, b):
    return lax.dot_general(
        a, b, (((1,), (0,)), ((), ())), preferred_element_type=jnp.float32
    )


HBM = pl.BlockSpec(memory_space=pltpu.HBM)
VMEM = pl.BlockSpec(memory_space=pltpu.VMEM)


def call(kernel, outs, scratch, flops, *args, in_hbm=(), out_hbm=()):
    shapes = [jax.ShapeDtypeStruct(s, jnp.float32) for s in outs]
    moved = sum(x.size for x in list(args) + shapes) * 4
    return pl.pallas_call(
        kernel,
        out_shape=shapes,
        in_specs=[HBM if k in in_hbm else VMEM for k in range(len(args))],
        out_specs=[HBM if k in out_hbm else VMEM for k in range(len(outs))],
        scratch_shapes=[pltpu.VMEM(s, jnp.float32) if isinstance(s, tuple) else s for s in scratch],
        compiler_params=pltpu.CompilerParams(vmem_limit_bytes=40 * 1024 * 1024),
        cost_estimate=pl.CostEstimate(flops=flops, bytes_accessed=moved, transcendentals=0),
    )(*args)


def pack_kernel(v_ref, out_ref):
    first = [jnp.concatenate([v_ref[0, i], v_ref[1, i][:, :32]], axis=1) for i in range(8)]
    rest = [v_ref[1, i][:, 32:] for i in range(8)]
    parts = []
    for h in range(2):
        parts += [first[2 * j + h] for j in range(4)]
        parts += [
            jnp.concatenate([rest[2 * j + h], rest[2 * j + 4 + h]], axis=1) for j in range(2)
        ]
    out_ref[...] = jnp.concatenate(parts, axis=0)


def fetch(hbm_ref, a_ref, sem, pieces):
    rows = a_ref.shape[0] // pieces
    copies = []
    for k in range(pieces):
        at = pl.ds(k * rows, rows)
        copies.append(pltpu.make_async_copy(hbm_ref.at[at, :], a_ref.at[at, :], sem.at[k]))
        copies[-1].start()
    return copies


def image_kernel(hbm_ref, g_ref, own_ref, send_ref, va_ref, vb_ref, a_ref, sem):
    copies = fetch(hbm_ref, a_ref, sem, 8)
    for x in range(XS):
        for j in range(4):
            for h in range(2):
                for r in range(4):
                    to = pl.ds((2 * j + h) * 128 + x * 64 + r, 16, stride=4)
                    va_ref[to, :] = g_ref[
                        pl.ds(x * SLICE + h * PART + j * 4 + r, 16, stride=2 * SLICE), :
                    ]
        for j in range(2):
            for h in range(2):
                for r in range(4):
                    both = g_ref[
                        pl.ds(x * SLICE + h * PART + 16 + j * 4 + r, 16, stride=2 * SLICE), :
                    ]
                    at = (2 * j + h) * 128 + x * 64 + r
                    vb_ref[pl.ds(at, 16, stride=4), :] = both
                    vb_ref[pl.ds(at + 512, 16, stride=4), :] = pltpu.roll(both, 64, 1)
    q = 0.0
    gram = 0.0
    for c in range(4):
        at = slice(c * 256, c * 256 + 256)
        v = jnp.concatenate([va_ref[at, :], vb_ref[at, :64]], axis=1)
        left = left_parts(v.T)
        gram = gram + plain(left[:W], right_parts(v[:, W:]))
        copies[2 * c].wait()
        copies[2 * c + 1].wait()
        tiles = [a_ref[pl.ds(c * 1024 + j, 256, stride=4), :] for j in range(4)]
        q = q + plain(left, right_parts(jnp.concatenate(tiles, axis=1)))
    for j in range(4):
        for kk in range(12):
            send_ref[pl.ds(kk * 4 + j, 16, stride=SEND), :] = q[
                kk * 16 : kk * 16 + 16, j * 128 : j * 128 + 128
            ]
    gram = jnp.concatenate([gram, jnp.zeros((W, 32), jnp.float32)], axis=1)
    for k in range(8):
        rows = gram[k * 16 : k * 16 + 16] if k < 6 else jnp.zeros((16, LANES), jnp.float32)
        send_ref[pl.ds(SLICE + k, 16, stride=SEND), :] = rows
    own = own_ref[...]
    for k in range(ROWS):
        send_ref[k * SEND + MINE : k * SEND + SEND, :] = own


def slice_kernel(r_ref, block_ref, y_ref, va_ref, vb_ref, sum_ref):
    total = r_ref[0:MINE, :]
    for k in range(1, ROWS):
        total = total + r_ref[k * SEND : k * SEND + MINE, :]
    sum_ref[...] = total
    for x in range(XS):
        for j in range(4):
            for r in range(4):
                va_ref[pl.ds(j * 128 + x * 64 + r, 16, stride=4), :] = r_ref[
                    pl.ds(MINE + x * 24 + j * 4 + r, 16, stride=SEND), :
                ]
        for j in range(2):
            for r in range(4):
                both = r_ref[pl.ds(MINE + 16 + x * 24 + j * 4 + r, 16, stride=SEND), :]
                vb_ref[pl.ds(j * 128 + x * 64 + r, 16, stride=4), :] = both
                vb_ref[pl.ds((j + 2) * 128 + x * 64 + r, 16, stride=4), :] = pltpu.roll(both, 64, 1)
    v = jnp.concatenate([va_ref[...], vb_ref[:, :64]], axis=1)
    y = jnp.concatenate([sum_ref[pl.ds(j, 12, stride=4), :] for j in range(4)], axis=1)
    ht = dot(y, v)
    low = jnp.concatenate([ht[0:6, LANES:], ht[6:12, W : W + 64]], axis=1)
    end = ht[6:12, W + 64 :]
    none = jnp.zeros((1, 32), jnp.float32)
    ends = [
        jnp.concatenate([end[k : k + 1], end[k + 1 : k + 2], end[k + 2 : k + 3], none], axis=1)
        for k in (0, 3)
    ]
    block_ref[0:48, :] = total[:SLICE]
    block_ref[48:64, :] = jnp.concatenate(
        [ht[0:6, :LANES], low] + ends + [jnp.zeros((2, LANES), jnp.float32)], axis=0
    )
    for k in range(ROWS):
        y_ref[k] = total


def turn_kernel(r_ref, out_ref):
    tail = r_ref[0, 48:BLOCK, :]
    for k in range(1, ZS):
        tail = tail + r_ref[k, 48:BLOCK, :]
    for k in range(ROWS):
        for x in range(XS):
            out_ref[2 * k + x, 0:48, :] = r_ref[k, 0:48, :]
            out_ref[2 * k + x, 48:BLOCK, :] = tail


def update_kernel(
    hbm_ref, vra_ref, vrb_ref, vca_ref, vcb_ref, y_ref, r_ref, t_ref, to_ref,
    a_ref, out_ref, yr_ref, yc_ref, left_ref, sem, out_sem,
):
    copies = fetch(hbm_ref, a_ref, sem, 4)

    def both(start):
        here = r_ref[pl.ds(start, 16, stride=2 * BLOCK), :]
        return here + r_ref[pl.ds(start + BLOCK, 16, stride=2 * BLOCK), :]

    def mul(a, b):
        (a1, a2), (b1, b2) = parts(a), parts(b)
        return plain(a1, b1) + plain(a2, b1) + plain(a1, b2)

    wide = jnp.concatenate([both(48 + k) for k in range(6)], axis=0)
    low = jnp.concatenate([both(54 + k) for k in range(6)], axis=0)
    ends = [both(60 + k) for k in range(2)]
    end = jnp.concatenate(
        [ends[k // 3][:, k % 3 * 32 : k % 3 * 32 + 32] for k in range(6)], axis=0
    )
    h11 = wide[:, :W]
    h12 = jnp.concatenate([wide[:, W:], low[:, :64]], axis=1)
    h22 = jnp.concatenate([low[:, 64:], end], axis=1)
    g = [y_ref[pl.ds(SLICE + k, 16, stride=MINE), :] for k in range(6)]
    g = jnp.concatenate(g, axis=0)[:, :W]
    t1 = t_ref[0]
    t2 = t_ref[1]
    t1t = t1.T
    tg = mul(t1, g)
    inner = h12 - 0.5 * mul(h11, tg)
    shift1 = 0.5 * mul(t1t, mul(h11, t1))
    crossed = mul(t1t, inner)
    fold = mul(tg.T, inner)
    second = h22 - fold - fold.T
    shift2 = 0.5 * mul(t2.T, mul(second, t2))
    corner = mul(crossed, t2) - mul(shift1, mul(g, t2))
    none = jnp.zeros((W, W), jnp.float32)
    left = jnp.concatenate(
        [
            jnp.concatenate([t1, -mul(tg, t2)], axis=1),
            jnp.concatenate([none, t2], axis=1),
        ],
        axis=0,
    )
    sym = jnp.concatenate(
        [
            jnp.concatenate([shift1 + shift1.T, corner], axis=1),
            jnp.concatenate([corner.T, shift2 + shift2.T], axis=1),
        ],
        axis=0,
    )
    for k in range(12):
        for j in range(4):
            for x in range(XS):
                i = 2 * j + x
                yr_ref[k * 16 : k * 16 + 16, i * 128 : i * 128 + 128] = r_ref[
                    pl.ds(x * BLOCK + k * 4 + j, 16, stride=2 * BLOCK), :
                ]
            yc_ref[k * 16 : k * 16 + 16, j * 128 : j * 128 + 128] = y_ref[
                pl.ds(k * 4 + j, 16, stride=MINE), :
            ]
    for i in range(4):
        at = slice(i * 256, i * 256 + 256)
        y = yr_ref[:, at].T
        rows = jnp.concatenate(
            [vra_ref[at, :], y[:, :128], vrb_ref[at, :64], y[:, 128:]], axis=1
        )
        left_ref[at, :] = left_parts(rows)
    vc = jnp.concatenate([vca_ref[...], vcb_ref[:, :64]], axis=1).T
    m1 = mul(left.T, yc_ref[...]) - mul(sym, vc)
    m2 = mul(left, vc)
    right = right_parts(jnp.concatenate([m1[:128], m2[:128], m1[128:], m2[128:]], axis=0))
    for copy in copies:
        copy.wait()
    outs = []
    for i in range(4):
        at = i * 256
        change = plain(left_ref[at : at + 256, :], right)
        for j in range(4):
            where = pl.ds(at * 4 + j, 256, stride=4)
            out_ref[where, :] = a_ref[where, :] - change[:, j * 128 : j * 128 + 128]
        part = pl.ds(at * 4, 1024)
        outs.append(pltpu.make_async_copy(out_ref.at[part, :], to_ref.at[part, :], out_sem.at[i]))
        outs[-1].start()
    for copy in outs:
        copy.wait()


def spread(array, axes):
    return lax.all_to_all(array, axes, split_axis=0, concat_axis=0, tiled=True)


def shards(matrix, vectors, factors):
    blocks = pltpu.with_memory_space_constraint(matrix.reshape(-1, LANES), pltpu.HBM)
    every = [(p, x, z) for p in range(ROWS) for x in range(XS) for z in range(ZS)]
    number = {at: k for k, at in enumerate(every)}
    same = [(number[p, x, z], number[z, x, p]) for p, x, z in every]
    whole = ("row", "xh", "z")

    (packed,) = call(pack_kernel, [(SLICE, LANES)], [], 0, vectors.reshape(2, 8, 4, W))
    pair = lax.all_gather(packed, "xh")
    own = lax.dynamic_slice_in_dim(pair, lax.axis_index("xh") * PART, PART, axis=1)
    own = lax.ppermute(own.reshape(SLICE, LANES), whole, same)
    gathered = lax.all_gather(pair.reshape(2 * SLICE, LANES), "z", axis=0, tiled=True)
    image, vra, vrb = call(
        image_kernel,
        [(ROWS * SEND, LANES), (1024, LANES), (1024, LANES)],
        [(4096, LANES), pltpu.SemaphoreType.DMA((8,))],
        2 * 1024 * 512 * 192,
        blocks,
        gathered,
        own,
        in_hbm=(0,),
    )
    image = spread(image.reshape(ROWS, SEND, LANES), "row").reshape(-1, LANES)
    block, mine, vca, vcb = call(
        slice_kernel,
        [(BLOCK, LANES), (ROWS, MINE, LANES), (512, LANES), (512, LANES)],
        [(MINE, LANES)],
        2 * 512 * 192 * 96,
        image,
    )
    y_cols = spread(mine, "row").reshape(-1, LANES)
    block = lax.all_gather(block, "z")
    (block,) = call(turn_kernel, [(2 * ROWS, BLOCK, LANES)], [], 0, block)
    y_rows = spread(block, ("row", "xh")).reshape(-1, LANES)
    (out,) = call(
        update_kernel,
        [(4096, LANES)],
        [
            (4096, LANES),
            (4096, LANES),
            (192, 1024),
            (192, 512),
            pltpu.VMEM((1024, 1152), jnp.bfloat16),
            pltpu.SemaphoreType.DMA((4,)),
            pltpu.SemaphoreType.DMA((4,)),
        ],
        2 * 1024 * 512 * 384,
        blocks,
        vra,
        vrb,
        vca,
        vcb,
        y_cols,
        y_rows,
        factors,
        in_hbm=(0,),
        out_hbm=(0,),
    )
    return out.reshape(matrix.shape)


def solution(mesh):
    finer = Mesh(mesh.devices.reshape(ROWS, XS, ZS), ("row", "xh", "z"))
    cols = ("xh", "z")
    placed = (P(None, "row", None, None, cols, None), P(None, None, "row", cols, None), P())
    return jax.shard_map(
        shards,
        mesh=finer,
        in_specs=placed,
        out_specs=placed[0],
        check_vma=False,
    )
```

```python
import jax
import jax.numpy as jnp
from jax import lax
from jax.experimental import pallas as pl
from jax.experimental.pallas import tpu as pltpu
from jax.sharding import Mesh
from jax.sharding import PartitionSpec as P

ROWS = 16
ZS = 16
XS = 2
W = 96
LANES = 128
SLICE = 48
PART = 24
BLOCK = 64
MINE = 56
SEND = 104


def dot(a, b, ca=1, cb=0):
    return lax.dot_general(
        a,
        b,
        (((ca,), (cb,)), ((), ())),
        precision=lax.Precision.HIGHEST,
        preferred_element_type=jnp.float32,
    )


def parts(x):
    high = x.astype(jnp.bfloat16)
    return high, (x - high.astype(jnp.float32)).astype(jnp.bfloat16)


def left_parts(x):
    high, low = parts(x)
    return jnp.concatenate([high, low, high], axis=1)


def right_parts(x):
    high, low = parts(x)
    return jnp.concatenate([high, high, low], axis=0)


def plain(a, b):
    return lax.dot_general(
        a, b, (((1,), (0,)), ((), ())), preferred_element_type=jnp.float32
    )


HBM = pl.BlockSpec(memory_space=pltpu.HBM)
VMEM = pl.BlockSpec(memory_space=pltpu.VMEM)


def call(kernel, outs, scratch, flops, *args, in_hbm=(), out_hbm=()):
    shapes = [jax.ShapeDtypeStruct(s, jnp.float32) for s in outs]
    moved = sum(x.size for x in list(args) + shapes) * 4
    return pl.pallas_call(
        kernel,
        out_shape=shapes,
        in_specs=[HBM if k in in_hbm else VMEM for k in range(len(args))],
        out_specs=[HBM if k in out_hbm else VMEM for k in range(len(outs))],
        scratch_shapes=[pltpu.VMEM(s, jnp.float32) if isinstance(s, tuple) else s for s in scratch],
        compiler_params=pltpu.CompilerParams(vmem_limit_bytes=40 * 1024 * 1024),
        cost_estimate=pl.CostEstimate(flops=flops, bytes_accessed=moved, transcendentals=0),
    )(*args)


def pack_kernel(v_ref, out_ref):
    first = [jnp.concatenate([v_ref[0, i], v_ref[1, i][:, :32]], axis=1) for i in range(8)]
    rest = [v_ref[1, i][:, 32:] for i in range(8)]
    parts = []
    for h in range(2):
        parts += [first[2 * j + h] for j in range(4)]
        parts += [
            jnp.concatenate([rest[2 * j + h], rest[2 * j + 4 + h]], axis=1) for j in range(2)
        ]
    out_ref[...] = jnp.concatenate(parts, axis=0)


def fetch(hbm_ref, a_ref, sem, pieces):
    rows = a_ref.shape[0] // pieces
    copies = []
    for k in range(pieces):
        at = pl.ds(k * rows, rows)
        copies.append(pltpu.make_async_copy(hbm_ref.at[at, :], a_ref.at[at, :], sem.at[k]))
        copies[-1].start()
    return copies


def image_kernel(hbm_ref, g_ref, own_ref, send_ref, va_ref, vb_ref, a_ref, sem):
    copies = fetch(hbm_ref, a_ref, sem, 4)
    for x in range(XS):
        for j in range(4):
            for h in range(2):
                for r in range(4):
                    to = pl.ds((2 * j + h) * 128 + x * 64 + r, 16, stride=4)
                    va_ref[to, :] = g_ref[
                        pl.ds(x * SLICE + h * PART + j * 4 + r, 16, stride=2 * SLICE), :
                    ]
        for j in range(2):
            for h in range(2):
                for r in range(4):
                    both = g_ref[
                        pl.ds(x * SLICE + h * PART + 16 + j * 4 + r, 16, stride=2 * SLICE), :
                    ]
                    at = (2 * j + h) * 128 + x * 64 + r
                    vb_ref[pl.ds(at, 16, stride=4), :] = both
                    vb_ref[pl.ds(at + 512, 16, stride=4), :] = pltpu.roll(both, 64, 1)
    q = 0.0
    gram = 0.0
    for c in range(4):
        at = slice(c * 256, c * 256 + 256)
        v = jnp.concatenate([va_ref[at, :], vb_ref[at, :64]], axis=1)
        left = left_parts(v.T)
        gram = gram + plain(left[:W], right_parts(v[:, W:]))
        copies[c].wait()
        tiles = [a_ref[pl.ds(c * 1024 + j, 256, stride=4), :] for j in range(4)]
        q = q + plain(left, right_parts(jnp.concatenate(tiles, axis=1)))
    for j in range(4):
        for kk in range(12):
            send_ref[pl.ds(kk * 4 + j, 16, stride=SEND), :] = q[
                kk * 16 : kk * 16 + 16, j * 128 : j * 128 + 128
            ]
    gram = jnp.concatenate([gram, jnp.zeros((W, 32), jnp.float32)], axis=1)
    for k in range(8):
        rows = gram[k * 16 : k * 16 + 16] if k < 6 else jnp.zeros((16, LANES), jnp.float32)
        send_ref[pl.ds(SLICE + k, 16, stride=SEND), :] = rows
    own = own_ref[...]
    for k in range(ROWS):
        send_ref[k * SEND + MINE : k * SEND + SEND, :] = own


def slice_kernel(r_ref, block_ref, y_ref, va_ref, vb_ref, sum_ref):
    total = r_ref[0:MINE, :]
    for k in range(1, ROWS):
        total = total + r_ref[k * SEND : k * SEND + MINE, :]
    sum_ref[...] = total
    for x in range(XS):
        for j in range(4):
            for r in range(4):
                va_ref[pl.ds(j * 128 + x * 64 + r, 16, stride=4), :] = r_ref[
                    pl.ds(MINE + x * 24 + j * 4 + r, 16, stride=SEND), :
                ]
        for j in range(2):
            for r in range(4):
                both = r_ref[pl.ds(MINE + 16 + x * 24 + j * 4 + r, 16, stride=SEND), :]
                vb_ref[pl.ds(j * 128 + x * 64 + r, 16, stride=4), :] = both
                vb_ref[pl.ds((j + 2) * 128 + x * 64 + r, 16, stride=4), :] = pltpu.roll(both, 64, 1)
    v = jnp.concatenate([va_ref[...], vb_ref[:, :64]], axis=1)
    y = jnp.concatenate([sum_ref[pl.ds(j, 12, stride=4), :] for j in range(4)], axis=1)
    ht = dot(y, v)
    low = jnp.concatenate([ht[0:6, LANES:], ht[6:12, W : W + 64]], axis=1)
    end = ht[6:12, W + 64 :]
    none = jnp.zeros((1, 32), jnp.float32)
    ends = [
        jnp.concatenate([end[k : k + 1], end[k + 1 : k + 2], end[k + 2 : k + 3], none], axis=1)
        for k in (0, 3)
    ]
    block_ref[0:48, :] = total[:SLICE]
    block_ref[48:64, :] = jnp.concatenate(
        [ht[0:6, :LANES], low] + ends + [jnp.zeros((2, LANES), jnp.float32)], axis=0
    )
    for k in range(ROWS):
        y_ref[k] = total


def turn_kernel(r_ref, out_ref):
    tail = r_ref[0, 48:BLOCK, :]
    for k in range(1, ZS):
        tail = tail + r_ref[k, 48:BLOCK, :]
    for k in range(ROWS):
        for x in range(XS):
            out_ref[2 * k + x, 0:48, :] = r_ref[k, 0:48, :]
            out_ref[2 * k + x, 48:BLOCK, :] = tail


def update_kernel(
    hbm_ref, vra_ref, vrb_ref, vca_ref, vcb_ref, y_ref, r_ref, t_ref, to_ref,
    a_ref, out_ref, yr_ref, yc_ref, left_ref, sem, out_sem,
):
    copies = fetch(hbm_ref, a_ref, sem, 4)

    def both(start):
        here = r_ref[pl.ds(start, 16, stride=2 * BLOCK), :]
        return here + r_ref[pl.ds(start + BLOCK, 16, stride=2 * BLOCK), :]

    def times(a, b):
        return plain(a[0], b[0]) + plain(a[1], b[0]) + plain(a[0], b[1])

    def mul(a, b):
        return times(parts(a), parts(b))

    wide = jnp.concatenate([both(48 + k) for k in range(6)], axis=0)
    low = jnp.concatenate([both(54 + k) for k in range(6)], axis=0)
    ends = [both(60 + k) for k in range(2)]
    end = jnp.concatenate(
        [ends[k // 3][:, k % 3 * 32 : k % 3 * 32 + 32] for k in range(6)], axis=0
    )
    h11 = wide[:, :W]
    h12 = jnp.concatenate([wide[:, W:], low[:, :64]], axis=1)
    h22 = jnp.concatenate([low[:, 64:], end], axis=1)
    g = [y_ref[pl.ds(SLICE + k, 16, stride=MINE), :] for k in range(6)]
    g = jnp.concatenate(g, axis=0)[:, :W]
    t1 = t_ref[0]
    t2 = t_ref[1]
    t1t = t1.T
    tg = mul(t1, g)
    inner = h12 - 0.5 * mul(h11, tg)
    shift1 = 0.5 * mul(t1t, mul(h11, t1))
    crossed = mul(t1t, inner)
    fold = mul(tg.T, inner)
    second = h22 - fold - fold.T
    shift2 = 0.5 * mul(t2.T, mul(second, t2))
    corner = mul(crossed, t2) - mul(shift1, mul(g, t2))
    none = jnp.zeros((W, W), jnp.float32)
    left = jnp.concatenate(
        [
            jnp.concatenate([t1, -mul(tg, t2)], axis=1),
            jnp.concatenate([none, t2], axis=1),
        ],
        axis=0,
    )
    sym = jnp.concatenate(
        [
            jnp.concatenate([shift1 + shift1.T, corner], axis=1),
            jnp.concatenate([corner.T, shift2 + shift2.T], axis=1),
        ],
        axis=0,
    )
    for k in range(12):
        for j in range(4):
            for x in range(XS):
                i = 2 * j + x
                yr_ref[k * 16 : k * 16 + 16, i * 128 : i * 128 + 128] = r_ref[
                    pl.ds(x * BLOCK + k * 4 + j, 16, stride=2 * BLOCK), :
                ]
            yc_ref[k * 16 : k * 16 + 16, j * 128 : j * 128 + 128] = y_ref[
                pl.ds(k * 4 + j, 16, stride=MINE), :
            ]
    for i in range(4):
        at = slice(i * 256, i * 256 + 256)
        y = yr_ref[:, at].T
        rows = jnp.concatenate(
            [vra_ref[at, :], y[:, :128], vrb_ref[at, :64], y[:, 128:]], axis=1
        )
        left_ref[at, :] = left_parts(rows)
    vc = parts(jnp.concatenate([vca_ref[...], vcb_ref[:, :64]], axis=1).T)
    m1 = mul(left.T, yc_ref[...]) - times(parts(sym), vc)
    m2 = times(parts(left), vc)
    right = right_parts(jnp.concatenate([m1[:128], m2[:128], m1[128:], m2[128:]], axis=0))
    for copy in copies:
        copy.wait()
    outs = []
    for i in range(4):
        at = i * 256
        change = plain(left_ref[at : at + 256, :], right)
        for j in range(4):
            where = pl.ds(at * 4 + j, 256, stride=4)
            out_ref[where, :] = a_ref[where, :] - change[:, j * 128 : j * 128 + 128]
        part = pl.ds(at * 4, 1024)
        outs.append(pltpu.make_async_copy(out_ref.at[part, :], to_ref.at[part, :], out_sem.at[i]))
        outs[-1].start()
    for copy in outs:
        copy.wait()


def spread(array, axes):
    return lax.all_to_all(array, axes, split_axis=0, concat_axis=0, tiled=True)


def shards(matrix, vectors, factors):
    blocks = pltpu.with_memory_space_constraint(matrix.reshape(-1, LANES), pltpu.HBM)
    every = [(p, x, z) for p in range(ROWS) for x in range(XS) for z in range(ZS)]
    number = {at: k for k, at in enumerate(every)}
    same = [(number[p, x, z], number[z, x, p]) for p, x, z in every]
    whole = ("row", "xh", "z")

    (packed,) = call(pack_kernel, [(SLICE, LANES)], [], 0, vectors.reshape(2, 8, 4, W))
    pair = lax.all_gather(packed, "xh")
    own = lax.dynamic_slice_in_dim(pair, lax.axis_index("xh") * PART, PART, axis=1)
    own = lax.ppermute(own.reshape(SLICE, LANES), whole, same)
    gathered = lax.all_gather(pair.reshape(2 * SLICE, LANES), "z", axis=0, tiled=True)
    image, vra, vrb = call(
        image_kernel,
        [(ROWS * SEND, LANES), (1024, LANES), (1024, LANES)],
        [(4096, LANES), pltpu.SemaphoreType.DMA((4,))],
        2 * 1024 * 512 * 192,
        blocks,
        gathered,
        own,
        in_hbm=(0,),
    )
    image = spread(image.reshape(ROWS, SEND, LANES), "row").reshape(-1, LANES)
    block, mine, vca, vcb = call(
        slice_kernel,
        [(BLOCK, LANES), (ROWS, MINE, LANES), (512, LANES), (512, LANES)],
        [(MINE, LANES)],
        2 * 512 * 192 * 96,
        image,
    )
    y_cols = spread(mine, "row").reshape(-1, LANES)
    block = lax.all_gather(block, "z")
    (block,) = call(turn_kernel, [(2 * ROWS, BLOCK, LANES)], [], 0, block)
    y_rows = spread(block, ("row", "xh")).reshape(-1, LANES)
    (out,) = call(
        update_kernel,
        [(4096, LANES)],
        [
            (4096, LANES),
            (4096, LANES),
            (192, 1024),
            (192, 512),
            pltpu.VMEM((1024, 1152), jnp.bfloat16),
            pltpu.SemaphoreType.DMA((4,)),
            pltpu.SemaphoreType.DMA((4,)),
        ],
        2 * 1024 * 512 * 384,
        blocks,
        vra,
        vrb,
        vca,
        vcb,
        y_cols,
        y_rows,
        factors,
        in_hbm=(0,),
        out_hbm=(0,),
    )
    return out.reshape(matrix.shape)


def solution(mesh):
    finer = Mesh(mesh.devices.reshape(ROWS, XS, ZS), ("row", "xh", "z"))
    cols = ("xh", "z")
    placed = (P(None, "row", None, None, cols, None), P(None, None, "row", cols, None), P())
    return jax.shard_map(
        shards,
        mesh=finer,
        in_specs=placed,
        out_specs=placed[0],
        check_vma=False,
    )
```
